32 devices in a mesh: groups: 2 (over x), ctx: 16 (over z, y, core).
Axes of the slice: x: 2, y: 2, z: 4, core: 2. Of those that a mesh axis runs over, the one named last changes fastest.
Arguments:
- hidden: bfloat16 [4096, 4096], P(('groups', 'ctx')), parts along dimension 0, may hold values from -6 to 6
- queries: bfloat16 [4096, 4096], P(('groups', 'ctx')), parts along dimension 0, may hold values from -64 to 64
- cache_weight: bfloat16 [4096, 1024], P('ctx'), may hold values from -0.09375 to 0.09375
- pattern: int32 [32, 7], P('groups'), parts along dimension 0, may hold values from -1 to 15, as said below
- span_pairs: int32 [32], P('groups'), parts along dimension 0, may hold values from 0 to 15, each once
Outputs:
- attended: bfloat16 [4096, 4096], P(('groups', 'ctx')), parts along dimension 0
The draws below stay inside these ranges and needn't reach their ends.
There are 2 independent parts, one for each index of `groups`. The reference program is written for one: setup_inputs(seed, part) draws one part's arguments, and reference() takes and returns one part's arrays. A program takes and returns all parts, laid end to end along the dimension named above; an argument that names none is the same for every part. Nothing has to cross between parts.
Inputs may be any that keep to these rules, and one draw needn't show every extreme that they name: `pattern`: row b lists b, b - 1, and so on down to max(0, b - 3), then, in rising order, the blocks below b - 3 that leave the same remainder, drawn for the row, modulo 4; the remaining entries are -1. `span_pairs`: A permutation.
All inputs are finite; a program needn't handle non-finite values.
Results may differ from the reference program's by a relative error of at most 0.004.
The reference program's roundings to bfloat16 on the way (of `key_rows`, `values`, `rotated` and `weights`) count: a program that leaves them out, or rounds other values in their place, can miss the bound.
Values may be sent and summed in bfloat16 or wider, within the bound.
A program may use at most 192 MiB of HBM per device.

```python
import jax
import jax.numpy as jnp
from jax import lax

D = 4096
QH = 32
KVH = 4
HD = 128
BLOCK = 128
WINDOW = 4
STRIDE = 4
T_DEV = 128
TOKENS = 2048
NB = 16
MAXK = 7
PAIRS = 16
N_CTX = 16


def draw_queries(key, part):
    key = jax.random.fold_in(key, 11)
    key_entries = jax.random.fold_in(key, 1)
    entries = jnp.clip(jax.random.normal(key_entries, (TOKENS, QH * HD), jnp.float32), -6.0, 6.0)
    return entries.astype(jnp.bfloat16)


def draw_pattern(key, part):
    key = jax.random.fold_in(key, 23)
    phases = jax.random.randint(key, (NB, 1), 0, STRIDE, dtype=jnp.int32)
    row_ids = jnp.arange(NB, dtype=jnp.int32)[:, None]
    local_steps = jnp.arange(WINDOW, dtype=jnp.int32)[None, :]
    local_ids = row_ids - local_steps
    local_ids = jnp.where(local_ids >= 0, local_ids, -1)
    stride_steps = jnp.arange(MAXK - WINDOW, dtype=jnp.int32)[None, :]
    stride_ids = phases + STRIDE * stride_steps
    stride_ids = jnp.where(stride_ids < row_ids - WINDOW + 1, stride_ids, -1)
    return jnp.concatenate([local_ids, stride_ids], axis=1).astype(jnp.int32)


def block_scale(key, shape, shards, smallest, high):
    def one(dim, shards_of):
        draws = jax.random.uniform(jax.random.fold_in(jax.random.fold_in(key, 6), dim), (shards_of,), jnp.float32, smallest / len(shards), high / len(shards))
        return jnp.repeat(jnp.exp(draws), shape[dim] // shards_of).reshape((-1,) + (1,) * (len(shape) - dim - 1))

    loudness = one(*shards[0])
    for cut in shards[1:]:
        loudness = loudness * one(*cut)
    return loudness


def gaussian(own_key, shape, scale, reach, pieces=(), kind=jnp.bfloat16):
    gain = block_scale(own_key, shape, pieces, -0.22, 0.18) if pieces else 1.0
    result = jax.random.normal(own_key, shape, jnp.float32) * scale * gain
    return jnp.minimum(jnp.maximum(result, -reach), reach).astype(kind)


def setup_inputs(seed: int = 0, part: int = 0) -> dict:
    seeds = jax.random.split(jax.random.key(seed), 6)
    part_keys = jax.random.split(jax.random.fold_in(seeds[5], part), 6)
    return {
        "hidden": gaussian(part_keys[0], (TOKENS, D), 1.0, 6.0, ((0, 16),)),
        "queries": draw_queries(jax.random.fold_in(jax.random.fold_in(seeds[5], part), 71), part),
        "cache_weight": gaussian(seeds[2], (D, 2 * KVH * HD), D ** -0.5, 0.09375, ((0, 16),)),
        "pattern": draw_pattern(jax.random.fold_in(jax.random.fold_in(seeds[5], part), 71), part),
        "span_pairs": jax.random.permutation(part_keys[4], PAIRS).astype(jnp.int32),
    }


ROPE_BASE = 500000.0
MASKED = -1e30


def rotary(values, positions, head_count, head_size):
    half_size = head_size // 2
    frequency = ROPE_BASE ** (-(jnp.arange(half_size, dtype=jnp.float32) * 2.0 / head_size))
    angles = positions.astype(jnp.float32)[:, None] * frequency[None, :]
    cosine = jnp.cos(angles)[:, None, :]
    sine_part = jnp.sin(angles)[:, None, :]
    shaped = values.reshape(values.shape[0], head_count, head_size)
    front_part = shaped[..., :half_size]
    back_part = shaped[..., half_size:]
    turned = jnp.concatenate([front_part * cosine - back_part * sine_part, back_part * cosine + front_part * sine_part], axis=-1)
    return turned.reshape(values.shape[0], head_count * head_size)


def stored_positions(span_pairs, rows_per_device, device_count):
    span_size = rows_per_device // 2
    low_span = span_pairs.astype(jnp.int32)
    high_span = 2 * device_count - 1 - low_span
    span_order = jnp.stack([low_span, high_span], axis=1).reshape(-1)
    offsets = jnp.arange(span_size, dtype=jnp.int32)
    return (span_order[:, None] * span_size + offsets[None, :]).reshape(-1)


def reference(hidden, queries, cache_weight, pattern, span_pairs):
    positions = stored_positions(span_pairs, T_DEV, N_CTX)
    cache_width = KVH * HD
    group_size = QH // KVH
    projected = jnp.dot(hidden, cache_weight, preferred_element_type=jnp.float32)
    key_rows = rotary(projected[:, :cache_width], positions, KVH, HD).astype(jnp.bfloat16)
    values = projected[:, cache_width:].astype(jnp.bfloat16)
    rotated = rotary(queries.astype(jnp.float32), positions, QH, HD).astype(jnp.bfloat16)
    block_ids = jnp.arange(NB, dtype=jnp.int32)
    listed = jnp.any(pattern[:, :, None] == block_ids[None, None, :], axis=1)
    key_wide = key_rows.astype(jnp.float32).reshape(TOKENS, KVH, HD)
    value_wide = values.astype(jnp.float32).reshape(TOKENS, KVH, HD)
    key_blocks = positions // BLOCK
    row_count = BLOCK

    def one_block(block_index):
        row_start = block_index * row_count
        query_rows = lax.dynamic_slice_in_dim(rotated, row_start, row_count, 0).astype(jnp.float32)
        query_rows = query_rows.reshape(row_count, KVH, group_size, HD)
        query_pos = lax.dynamic_slice_in_dim(positions, row_start, row_count, 0)
        scores = jnp.einsum("rhgd,khd->rhgk", query_rows, key_wide) * (HD ** -0.5)
        allowed = listed[query_pos // BLOCK][:, key_blocks] & (positions[None, :] <= query_pos[:, None])
        allowed = allowed[:, None, None, :]
        masked = jnp.where(allowed, scores, MASKED)
        row_peak = jnp.max(masked, axis=-1, keepdims=True)
        weights = jnp.where(allowed, jnp.exp(masked - row_peak), 0.0).astype(jnp.bfloat16)
        weights = lax.optimization_barrier(weights).astype(jnp.float32)
        totals = jnp.sum(weights, axis=-1, keepdims=True)
        mixed_rows = jnp.einsum("rhgk,khd->rhgd", weights, value_wide) / totals
        return mixed_rows.reshape(row_count, QH * HD).astype(jnp.bfloat16)

    outputs = lax.map(one_block, jnp.arange(TOKENS // row_count, dtype=jnp.int32))
    return outputs.reshape(TOKENS, QH * HD)
```

```python
import functools
import math

import jax
import jax.numpy as jnp
from jax import lax
from jax.experimental import pallas as pl
from jax.experimental.pallas import tpu as pltpu
from jax.sharding import PartitionSpec as P

QH = 32
KVH = 4
HD = 128
BLOCK = 128
ROPE_BASE = 500000.0
MASKED = -1e30
CHUNK = 2 * BLOCK


def rope_tables(positions):
    half = HD // 2
    frequency = ROPE_BASE ** (-(jnp.arange(half, dtype=jnp.float32) * 2.0 / HD))
    angles = positions.astype(jnp.float32)[:, None] * frequency[None, :]
    cosine, sine = jnp.cos(angles), jnp.sin(angles)
    return (
        jnp.concatenate([cosine, cosine], axis=1),
        jnp.concatenate([-sine, sine], axis=1),
    )


def attend_kernel(
    n, pattern_ref, spans_ref, rot_ref, kv_ref, out_ref, kbuf, vbuf, scores, owner
):
    me = lax.axis_index("ctx")
    tok_rows = out_ref.shape[0]
    span = tok_rows // 2
    width = kv_ref.shape[2]
    group = QH // KVH
    rows = group * span
    slots = pattern_ref.shape[1]
    factor = HD ** (-0.5) * math.log2(math.e)

    def place(d, carry):
        owner[spans_ref[d]] = d
        return carry

    lax.fori_loop(0, n, place, 0)
    vbuf[:, :, HD:] = jnp.ones_like(vbuf[:, :, HD:])
    low = spans_ref[me]

    for part in range(2):
        span_id = low if part == 0 else 2 * n - 1 - low
        query_block = span_id * span // BLOCK
        offset = span_id * span - query_block * BLOCK

        def fill(i, count):
            block = pattern_ref[query_block, i]

            @pl.when(block >= 0)
            def _():
                for e in range(2):
                    unit = 2 * block + e
                    upper = unit >= n
                    device = owner[jnp.where(upper, 2 * n - 1 - unit, unit)]
                    row = pl.multiple_of(device * tok_rows + jnp.where(upper, span, 0), span)
                    to = pl.ds(pl.multiple_of(count * BLOCK + e * span, span), span)
                    for h in range(KVH):
                        for buf, col in ((kbuf, h * HD), (vbuf, (KVH + h) * HD)):
                            buf[h, to, :HD] = kv_ref[
                                col // width, pl.ds(row, span), col % width : col % width + HD
                            ]

            return count + (block >= 0).astype(jnp.int32)

        count = lax.fori_loop(0, slots, fill, jnp.int32(0))

        @pl.when(count % 2 == 1)
        def _():
            to = pl.ds(pl.multiple_of(count * BLOCK, BLOCK), BLOCK)
            kbuf[:, to, :] = jnp.zeros((KVH, BLOCK, HD), kbuf.dtype)
            vbuf[:, to, :HD] = jnp.zeros((KVH, BLOCK, HD), vbuf.dtype)

        chunks = (count + 1) // 2

        for h in range(KVH):
            query = rot_ref[part, h * group : (h + 1) * group].reshape(rows, HD)

            def score(c, peak):
                keys = kbuf[h, pl.ds(pl.multiple_of(c * CHUNK, CHUNK), CHUNK), :]
                s = lax.dot_general(
                    query, keys, (((1,), (1,)), ((), ())), preferred_element_type=jnp.float32
                )
                col = c * CHUNK + lax.broadcasted_iota(jnp.int32, (span, CHUNK), 1)
                line = offset + lax.broadcasted_iota(jnp.int32, (span, CHUNK), 0)
                live = (col < count * BLOCK) & ((col >= BLOCK) | (col <= line))
                bias = jnp.where(live, 0.0, MASKED)
                s = (s.reshape(group, span, CHUNK) + bias[None]).reshape(rows, CHUNK)
                scores[c] = s
                return jnp.maximum(peak, jnp.maximum(s[:, :BLOCK], s[:, BLOCK:]))

            peak = lax.fori_loop(
                0, chunks, score, jnp.full((rows, BLOCK), MASKED, jnp.float32)
            )
            top = jnp.max(peak, axis=1, keepdims=True)

            def mix(c, total):
                weights = jnp.exp2((scores[c] - top) * factor).astype(jnp.bfloat16)
                values = vbuf[h, pl.ds(pl.multiple_of(c * CHUNK, CHUNK), CHUNK), :]
                return total + jnp.dot(weights, values, preferred_element_type=jnp.float32)

            total = lax.fori_loop(0, chunks, mix, jnp.zeros((rows, 2 * HD), jnp.float32))
            result = (total[:, :HD] / total[:, HD:]).astype(jnp.bfloat16)
            for j in range(group):
                head = h * group + j
                out_ref[part * span : (part + 1) * span, head * HD : (head + 1) * HD] = result[
                    j * span : (j + 1) * span
                ]


def attend(n, pattern, span_pairs, rotated, kv, tok_rows):
    span = tok_rows // 2
    chunks = (pattern.shape[1] + 1) // 2
    keys = chunks * CHUNK
    rows = QH // KVH * span
    smem = pl.BlockSpec(memory_space=pltpu.SMEM)
    vmem = pl.BlockSpec(memory_space=pltpu.VMEM)
    return pl.pallas_call(
        functools.partial(attend_kernel, n),
        out_shape=jax.ShapeDtypeStruct((tok_rows, QH * HD), jnp.bfloat16),
        in_specs=[smem, smem, vmem, vmem],
        out_specs=vmem,
        scratch_shapes=[
            pltpu.VMEM((KVH, keys, HD), jnp.bfloat16),
            pltpu.VMEM((KVH, keys, 2 * HD), jnp.bfloat16),
            pltpu.VMEM((chunks, rows, CHUNK), jnp.float32),
            pltpu.SMEM((n,), jnp.int32),
        ],
        compiler_params=pltpu.CompilerParams(vmem_limit_bytes=52 * 1024 * 1024),
    )(pattern, span_pairs, rotated, kv)


def body(hidden, queries, cache_weight, pattern, span_pairs):
    tok_rows = hidden.shape[0]
    n = lax.axis_size("ctx")
    me = lax.axis_index("ctx")
    span = tok_rows // 2
    low = span_pairs[me]
    offsets = jnp.arange(span, dtype=jnp.int32)
    positions = jnp.concatenate([low * span + offsets, (2 * n - 1 - low) * span + offsets])
    cosine, sine = rope_tables(positions)

    def turn(x, heads):
        x = x.reshape(tok_rows, heads, HD)
        swapped = jnp.concatenate([x[..., HD // 2 :], x[..., : HD // 2]], axis=-1)
        return x * cosine[:, None] + swapped * sine[:, None]

    projected = jnp.dot(
        hidden,
        lax.all_gather(cache_weight, "ctx", axis=0, tiled=True),
        preferred_element_type=jnp.float32,
    )
    keys = turn(projected[:, : KVH * HD], KVH).reshape(tok_rows, KVH * HD)
    local = jnp.concatenate([keys, projected[:, KVH * HD :]], axis=1).astype(jnp.bfloat16)
    kv = lax.all_gather(local, "ctx", axis=0, tiled=True)[None]
    rotated = turn(queries.astype(jnp.float32), QH).astype(jnp.bfloat16)
    rotated = rotated.reshape(2, span, QH, HD).transpose(0, 2, 1, 3)
    return attend(n, pattern, span_pairs, rotated, kv, tok_rows)


def solution(mesh):
    in_specs = (
        P(("groups", "ctx"), None),
        P(("groups", "ctx"), None),
        P("ctx", None),
        P("groups", None),
        P("groups"),
    )
    return jax.shard_map(
        body,
        mesh=mesh,
        in_specs=in_specs,
        out_specs=P(("groups", "ctx"), None),
        check_vma=False,
    )
```

```python
import functools
import math

import jax
import jax.numpy as jnp
from jax import lax
from jax.experimental import pallas as pl
from jax.experimental.pallas import tpu as pltpu
from jax.sharding import PartitionSpec as P

QH = 32
KVH = 4
HD = 128
BLOCK = 128
ROPE_BASE = 500000.0
MASKED = -1e30
CHUNK = 2 * BLOCK


def rope_tables(positions):
    half = HD // 2
    frequency = ROPE_BASE ** (-(jnp.arange(half, dtype=jnp.float32) * 2.0 / HD))
    angles = positions.astype(jnp.float32)[:, None] * frequency[None, :]
    cosine, sine = jnp.cos(angles), jnp.sin(angles)
    return (
        jnp.concatenate([cosine, cosine], axis=1),
        jnp.concatenate([-sine, sine], axis=1),
    )


def attend_kernel(
    n, pattern_ref, spans_ref, rot_ref, kv_ref, out_ref, kbuf, vbuf, scores, owner
):
    me = lax.axis_index("ctx")
    tok_rows = out_ref.shape[0]
    span = tok_rows // 2
    width = kv_ref.shape[2]
    group = QH // KVH
    rows = group * span
    slots = pattern_ref.shape[1]
    factor = HD ** (-0.5) * math.log2(math.e)

    def place(d, carry):
        owner[spans_ref[d]] = d
        return carry

    lax.fori_loop(0, n, place, 0)
    vbuf[:, :, HD:] = jnp.ones_like(vbuf[:, :, HD:])
    low = spans_ref[me]

    for part in range(2):
        span_id = low if part == 0 else 2 * n - 1 - low
        query_block = span_id * span // BLOCK
        offset = span_id * span - query_block * BLOCK

        def fill(i, count):
            block = pattern_ref[query_block, i]

            @pl.when(block >= 0)
            def _():
                for e in range(2):
                    unit = 2 * block + e
                    upper = unit >= n
                    device = owner[jnp.where(upper, 2 * n - 1 - unit, unit)]
                    row = pl.multiple_of(device * tok_rows + jnp.where(upper, span, 0), span)
                    to = pl.ds(pl.multiple_of(count * BLOCK + e * span, span), span)
                    for h in range(KVH):
                        for buf, col in ((kbuf, h * HD), (vbuf, (KVH + h) * HD)):
                            buf[h, to, :HD] = kv_ref[
                                col // width, pl.ds(row, span), col % width : col % width + HD
                            ]

            return count + (block >= 0).astype(jnp.int32)

        count = lax.fori_loop(0, slots, fill, jnp.int32(0))

        @pl.when(count % 2 == 1)
        def _():
            to = pl.ds(pl.multiple_of(count * BLOCK, BLOCK), BLOCK)
            kbuf[:, to, :] = jnp.zeros((KVH, BLOCK, HD), kbuf.dtype)
            vbuf[:, to, :HD] = jnp.zeros((KVH, BLOCK, HD), vbuf.dtype)

        chunks = (count + 1) // 2

        for h in range(KVH):
            query = rot_ref[part, h * group : (h + 1) * group].reshape(rows, HD)

            def score(c, peak):
                keys = kbuf[h, pl.ds(pl.multiple_of(c * CHUNK, CHUNK), CHUNK), :]
                s = lax.dot_general(
                    query, keys, (((1,), (1,)), ((), ())), preferred_element_type=jnp.float32
                )
                col = c * CHUNK + lax.broadcasted_iota(jnp.int32, (span, CHUNK), 1)
                line = offset + lax.broadcasted_iota(jnp.int32, (span, CHUNK), 0)
                live = (col < count * BLOCK) & ((col >= BLOCK) | (col <= line))
                bias = jnp.where(live, 0.0, MASKED)
                s = (s.reshape(group, span, CHUNK) + bias[None]).reshape(rows, CHUNK)
                scores[c] = s
                return jnp.maximum(peak, jnp.maximum(s[:, :BLOCK], s[:, BLOCK:]))

            peak = lax.fori_loop(
                0, chunks, score, jnp.full((rows, BLOCK), MASKED, jnp.float32)
            )
            top = jnp.max(peak, axis=1, keepdims=True)

            def mix(c, total):
                weights = jnp.exp2((scores[c] - top) * factor).astype(jnp.bfloat16)
                values = vbuf[h, pl.ds(pl.multiple_of(c * CHUNK, CHUNK), CHUNK), :]
                return total + jnp.dot(weights, values, preferred_element_type=jnp.float32)

            total = lax.fori_loop(0, chunks, mix, jnp.zeros((rows, 2 * HD), jnp.float32))
            result = (total[:, :HD] / total[:, HD:]).astype(jnp.bfloat16)
            for j in range(group):
                head = h * group + j
                out_ref[part * span : (part + 1) * span, head * HD : (head + 1) * HD] = result[
                    j * span : (j + 1) * span
                ]


def attend(n, pattern, span_pairs, rotated, kv, tok_rows):
    span = tok_rows // 2
    chunks = (pattern.shape[1] + 1) // 2
    keys = chunks * CHUNK
    rows = QH // KVH * span
    smem = pl.BlockSpec(memory_space=pltpu.SMEM)
    vmem = pl.BlockSpec(memory_space=pltpu.VMEM)
    return pl.pallas_call(
        functools.partial(attend_kernel, n),
        out_shape=jax.ShapeDtypeStruct((tok_rows, QH * HD), jnp.bfloat16),
        in_specs=[smem, smem, vmem, vmem],
        out_specs=vmem,
        scratch_shapes=[
            pltpu.VMEM((KVH, keys, HD), jnp.bfloat16),
            pltpu.VMEM((KVH, keys, 2 * HD), jnp.bfloat16),
            pltpu.VMEM((chunks, rows, CHUNK), jnp.float32),
            pltpu.SMEM((n,), jnp.int32),
        ],
        compiler_params=pltpu.CompilerParams(vmem_limit_bytes=52 * 1024 * 1024),
    )(pattern, span_pairs, rotated, kv)


MESH = pl.DeviceIdType.MESH
KBLOCK = 512


def project_kernel(
    n,
    groups,
    weight_ref,
    hidden_ref,
    queries_ref,
    table_ref,
    rot_ref,
    kv_ref,
    weights,
    states,
    asked,
    tables,
    product,
    outgoing,
    sems,
    kv_sems,
    side_sems,
    kv_side_sems,
    own_sems,
    kv_own_sems,
    peer_sems,
    table_sems,
    kv_peer_sems,
    local_sems,
):
    g = lax.axis_index("groups")
    me = lax.axis_index("ctx")
    chips = n // 2
    half = chips // 2
    chip, core = me // 2, me % 2
    depth, width = weight_ref.shape[0], weights.shape[1]
    tok_rows = hidden_ref.shape[0]
    span = tok_rows // 2
    cut = depth // 2

    if chips > 8:
        spot = chip
    else:
        spot = (1 - chip % 2) * (chip // 2) + (chip % 2) * (chips - 1 - chip // 2)

    def index(position, which):
        p = (position + chips) % chips
        if chips > 8:
            return p * 2 + which
        back = p // half
        return 2 * ((1 - back) * 2 * p + back * (2 * (chips - 1 - p) + 1)) + which

    sibling = (g, chip * 2 + 1 - core)
    ring = ((g, index(spot + 1, core)), (g, index(spot - 1, core)))
    peers = [((g + d) % groups, me) for d in range(1, groups)]

    barrier = pltpu.get_barrier_semaphore()
    for device in (sibling, *ring, *peers):
        pl.semaphore_signal(barrier, inc=1, device_id=device, device_id_type=MESH)
    pl.semaphore_wait(barrier, 3 + len(peers))

    started = []

    def copy(source, target, send, receive, device):
        return pltpu.make_async_remote_copy(
            src_ref=source,
            dst_ref=target,
            send_sem=send,
            recv_sem=receive,
            device_id=device,
            device_id_type=MESH,
        )

    def send(*args):
        c = copy(*args)
        c.start()
        started.append(c)

    def gather(place, first, pieces, ready, ring_sems, across, own, between):
        def used(d, k, i):
            if k < half - 1:
                return True
            return (i < pieces // 2) == (d == 0)

        for i in range(pieces):
            ready(i)
            for d in range(2):
                if used(d, 0, i):
                    send(
                        first(i), place(me, i), ring_sems.at[0, d, 0, i],
                        ring_sems.at[1, d, 0, i], ring[d],
                    )
            send(first(i), place(me, i), own.at[0, i], own.at[1, i], sibling)
        between()
        for k in range(1, half + 1):
            for i in range(pieces):
                for d in range(2):
                    if not used(d, k - 1, i):
                        continue
                    at = place(index(spot - k if d == 0 else spot + k, core), i)
                    s, r = ring_sems.at[0, d, k - 1, i], ring_sems.at[1, d, k - 1, i]
                    copy(at, at, s, r, ring[d]).wait_recv()
                    if k < half and used(d, k, i):
                        send(at, at, ring_sems.at[0, d, k, i], ring_sems.at[1, d, k, i], ring[d])
                    send(at, at, across.at[0, d, k - 1, i], across.at[1, d, k - 1, i], sibling)
        for i in range(pieces):
            at = place(sibling[1], i)
            copy(at, at, own.at[0, i], own.at[1, i], sibling).wait_recv()
        for k in range(1, half + 1):
            for i in range(pieces):
                for d in range(2):
                    if used(d, k - 1, i):
                        at = place(index(spot - k if d == 0 else spot + k, 1 - core), i)
                        s, r = across.at[0, d, k - 1, i], across.at[1, d, k - 1, i]
                        copy(at, at, s, r, sibling).wait_recv()

    columns = pl.ds(pl.multiple_of(g * width, width), width)

    def weight_place(slot, i):
        return weights.at[pl.ds(pl.multiple_of(slot * depth + i * cut, cut), cut), :]

    locals_ = [
        pltpu.make_async_copy(
            weight_ref.at[:, columns],
            weights.at[pl.ds(pl.multiple_of(me * depth, depth), depth), :],
            local_sems.at[0],
        ),
        pltpu.make_async_copy(hidden_ref, states.at[g], local_sems.at[1]),
        pltpu.make_async_copy(queries_ref, asked, local_sems.at[2]),
        pltpu.make_async_copy(table_ref, tables.at[g], local_sems.at[3]),
    ]

    def between():
        for d, device in enumerate(peers):
            send(hidden_ref, states.at[g], peer_sems.at[0, d], peer_sems.at[1, d], device)
            send(table_ref, tables.at[g], table_sems.at[0, d], table_sems.at[1, d], device)
        for c in locals_:
            c.start()
        for c in locals_:
            c.wait()

        def rotate(h, carry):
            x = asked[:, pl.ds(pl.multiple_of(h * HD, HD), HD)].astype(jnp.float32)
            y = x * tables[g, 0] + pltpu.roll(x, HD // 2, 1) * tables[g, 1]
            y = y.astype(jnp.bfloat16)
            rot_ref[0, h] = y[:span]
            rot_ref[1, h] = y[span:]
            return carry

        lax.fori_loop(0, QH, rotate, 0)

    gather(
        weight_place,
        lambda i: weight_ref.at[pl.ds(i * cut, cut), columns],
        2,
        lambda i: None,
        sems,
        side_sems,
        own_sems,
        between,
    )
    for d in range(groups - 1):
        source = (g + groups - 1 - d) % groups
        copy(
            states.at[source], states.at[source], peer_sems.at[0, d], peer_sems.at[1, d], peers[d]
        ).wait_recv()
        copy(
            tables.at[source], tables.at[source], table_sems.at[0, d], table_sems.at[1, d], peers[d]
        ).wait_recv()

    product[...] = jnp.zeros_like(product)

    def multiply(k, carry):
        at = pl.ds(pl.multiple_of(k * KBLOCK, KBLOCK), KBLOCK)
        x = states[:, :, at].reshape(groups * tok_rows, KBLOCK)
        product[...] += jnp.dot(
            x, weights[at, :], preferred_element_type=jnp.float32
        ).reshape(product.shape)
        return carry

    lax.fori_loop(0, states.shape[2] // KBLOCK, multiply, 0)

    is_key = g * width < KVH * HD

    def finish(which, store):
        for h in range(width // HD):
            x = product[which, :, h * HD : (h + 1) * HD]
            y = x * tables[which, 0] + pltpu.roll(x, HD // 2, 1) * tables[which, 1]
            store(h, jnp.where(is_key, y, x).astype(jnp.bfloat16))

    def store_own(h, value):
        kv_ref[g, me, :, h * HD : (h + 1) * HD] = value

    finish(g, store_own)

    def share():
        for d, device in enumerate(peers):

            def store(h, value, d=d):
                outgoing[d, :, h * HD : (h + 1) * HD] = value

            finish(device[0], store)
            send(
                outgoing.at[d], kv_ref.at[g, me], kv_peer_sems.at[0, d], kv_peer_sems.at[1, d],
                device,
            )

    def kv_place(slot, i):
        return kv_ref.at[(g + i) % groups, slot]

    def ready(i):
        if i == 1:
            share()
        if i:
            at = kv_place(me, i)
            d = groups - i - 1
            copy(at, at, kv_peer_sems.at[0, d], kv_peer_sems.at[1, d], peers[d]).wait_recv()

    gather(
        kv_place,
        lambda i: kv_place(me, i),
        groups,
        ready,
        kv_sems,
        kv_side_sems,
        kv_own_sems,
        lambda: None,
    )
    for c in started:
        c.wait_send()


def project(n, groups, weight, hidden, queries, table):
    depth, width = weight.shape[0], weight.shape[1] // groups
    tok_rows, wide = hidden.shape
    half = n // 4
    whole = pl.BlockSpec(memory_space=pl.ANY)
    vmem = pl.BlockSpec(memory_space=pltpu.VMEM)
    dma = pltpu.SemaphoreType.DMA
    return pl.pallas_call(
        functools.partial(project_kernel, n, groups),
        out_shape=(
            jax.ShapeDtypeStruct((2, QH, tok_rows // 2, HD), jnp.bfloat16),
            jax.ShapeDtypeStruct((groups, n, tok_rows, width), jnp.bfloat16),
        ),
        in_specs=[whole, whole, whole, whole],
        out_specs=(vmem, vmem),
        scratch_shapes=[
            pltpu.VMEM((n * depth, width), jnp.bfloat16),
            pltpu.VMEM((groups, tok_rows, wide), jnp.bfloat16),
            pltpu.VMEM(queries.shape, jnp.bfloat16),
            pltpu.VMEM((groups, *table.shape), jnp.float32),
            pltpu.VMEM((groups, tok_rows, width), jnp.float32),
            pltpu.VMEM((groups - 1, tok_rows, width), jnp.bfloat16),
            dma((2, 2, half, 2)),
            dma((2, 2, half, groups)),
            dma((2, 2, half, 2)),
            dma((2, 2, half, groups)),
            dma((2, 2)),
            dma((2, groups)),
            dma((2, groups - 1)),
            dma((2, groups - 1)),
            dma((2, groups - 1)),
            dma((4,)),
        ],
        compiler_params=pltpu.CompilerParams(
            collective_id=0, has_side_effects=True, vmem_limit_bytes=48 * 1024 * 1024
        ),
    )(weight, hidden, queries, table)


def body(groups, hidden, queries, cache_weight, pattern, span_pairs):
    tok_rows = hidden.shape[0]
    n = lax.axis_size("ctx")
    me = lax.axis_index("ctx")
    span = tok_rows // 2
    low = span_pairs[me]
    offsets = jnp.arange(span, dtype=jnp.int32)
    positions = jnp.concatenate([low * span + offsets, (2 * n - 1 - low) * span + offsets])
    table = jnp.stack(rope_tables(positions))
    rotated, kv = project(n, groups, cache_weight, hidden, queries, table)
    kv = kv.reshape(groups, n * tok_rows, kv.shape[3])
    return attend(n, pattern, span_pairs, rotated, kv, tok_rows)


def solution(mesh):
    in_specs = (
        P(("groups", "ctx"), None),
        P(("groups", "ctx"), None),
        P("ctx", None),
        P("groups", None),
        P("groups"),
    )
    return jax.shard_map(
        functools.partial(body, mesh.shape["groups"]),
        mesh=mesh,
        in_specs=in_specs,
        out_specs=P(("groups", "ctx"), None),
        check_vma=False,
    )
```

```python
import functools
import math

import jax
import jax.numpy as jnp
from jax import lax
from jax.experimental import pallas as pl
from jax.experimental.pallas import tpu as pltpu
from jax.sharding import PartitionSpec as P

QH = 32
KVH = 4
HD = 128
BLOCK = 128
ROPE_BASE = 500000.0
MASKED = -1e30
CHUNK = 2 * BLOCK


def attend_kernel(
    n, pattern_ref, spans_ref, rot_ref, kv_ref, out_ref, kbuf, vbuf, scores, owner
):
    me = lax.axis_index("ctx")
    tok_rows = out_ref.shape[0]
    span = tok_rows // 2
    width = kv_ref.shape[2]
    group = QH // KVH
    rows = group * span
    slots = pattern_ref.shape[1]
    factor = HD ** (-0.5) * math.log2(math.e)

    def place(d, carry):
        owner[spans_ref[d]] = d
        return carry

    lax.fori_loop(0, n, place, 0)
    vbuf[:, :, HD:] = jnp.ones_like(vbuf[:, :, HD:])
    low = spans_ref[me]

    for part in range(2):
        span_id = low if part == 0 else 2 * n - 1 - low
        query_block = span_id * span // BLOCK
        offset = span_id * span - query_block * BLOCK

        def fill(i, count):
            block = pattern_ref[query_block, i]

            @pl.when(block >= 0)
            def _():
                for e in range(2):
                    unit = 2 * block + e
                    upper = unit >= n
                    device = owner[jnp.where(upper, 2 * n - 1 - unit, unit)]
                    row = pl.multiple_of(device * tok_rows + jnp.where(upper, span, 0), span)
                    to = pl.ds(pl.multiple_of(count * BLOCK + e * span, span), span)
                    for h in range(KVH):
                        for buf, col in ((kbuf, h * HD), (vbuf, (KVH + h) * HD)):
                            buf[h, to, :HD] = kv_ref[
                                col // width, pl.ds(row, span), col % width : col % width + HD
                            ]

            return count + (block >= 0).astype(jnp.int32)

        count = lax.fori_loop(0, slots, fill, jnp.int32(0))

        @pl.when(count % 2 == 1)
        def _():
            to = pl.ds(pl.multiple_of(count * BLOCK, BLOCK), BLOCK)
            kbuf[:, to, :] = jnp.zeros((KVH, BLOCK, HD), kbuf.dtype)
            vbuf[:, to, :HD] = jnp.zeros((KVH, BLOCK, HD), vbuf.dtype)

        chunks = (count + 1) // 2

        for h in range(KVH):
            query = rot_ref[part, h * group : (h + 1) * group].reshape(rows, HD)

            def score(c, peak):
                keys = kbuf[h, pl.ds(pl.multiple_of(c * CHUNK, CHUNK), CHUNK), :]
                s = lax.dot_general(
                    query, keys, (((1,), (1,)), ((), ())), preferred_element_type=jnp.float32
                )
                col = c * CHUNK + lax.broadcasted_iota(jnp.int32, (span, CHUNK), 1)
                line = offset + lax.broadcasted_iota(jnp.int32, (span, CHUNK), 0)
                live = (col < count * BLOCK) & ((col >= BLOCK) | (col <= line))
                bias = jnp.where(live, 0.0, MASKED)
                s = (s.reshape(group, span, CHUNK) + bias[None]).reshape(rows, CHUNK)
                scores[c] = s
                return jnp.maximum(peak, jnp.maximum(s[:, :BLOCK], s[:, BLOCK:]))

            peak = lax.fori_loop(
                0, chunks, score, jnp.full((rows, BLOCK), MASKED, jnp.float32)
            )
            top = jnp.max(peak, axis=1, keepdims=True)

            def mix(c, total):
                weights = jnp.exp2((scores[c] - top) * factor).astype(jnp.bfloat16)
                values = vbuf[h, pl.ds(pl.multiple_of(c * CHUNK, CHUNK), CHUNK), :]
                return total + jnp.dot(weights, values, preferred_element_type=jnp.float32)

            total = lax.fori_loop(0, chunks, mix, jnp.zeros((rows, 2 * HD), jnp.float32))
            result = (total[:, :HD] / total[:, HD:]).astype(jnp.bfloat16)
            for j in range(group):
                head = h * group + j
                out_ref[part * span : (part + 1) * span, head * HD : (head + 1) * HD] = result[
                    j * span : (j + 1) * span
                ]


def attend(n, pattern, span_pairs, rotated, kv, tok_rows):
    span = tok_rows // 2
    chunks = (pattern.shape[1] + 1) // 2
    keys = chunks * CHUNK
    rows = QH // KVH * span
    smem = pl.BlockSpec(memory_space=pltpu.SMEM)
    vmem = pl.BlockSpec(memory_space=pltpu.VMEM)
    return pl.pallas_call(
        functools.partial(attend_kernel, n),
        out_shape=jax.ShapeDtypeStruct((tok_rows, QH * HD), jnp.bfloat16),
        in_specs=[smem, smem, vmem, vmem],
        out_specs=vmem,
        scratch_shapes=[
            pltpu.VMEM((KVH, keys, HD), jnp.bfloat16),
            pltpu.VMEM((KVH, keys, 2 * HD), jnp.bfloat16),
            pltpu.VMEM((chunks, rows, CHUNK), jnp.float32),
            pltpu.SMEM((n,), jnp.int32),
        ],
        compiler_params=pltpu.CompilerParams(vmem_limit_bytes=24 * 1024 * 1024),
    )(pattern, span_pairs, rotated, kv)


MESH = pl.DeviceIdType.MESH
KBLOCK = 512


def project_kernel(
    n,
    groups,
    weight_ref,
    hidden_ref,
    queries_ref,
    spans_ref,
    frequency_ref,
    rot_ref,
    kv_ref,
    weights,
    states,
    asked,
    tables,
    product,
    outgoing,
    sems,
    kv_sems,
    side_sems,
    kv_side_sems,
    own_sems,
    kv_own_sems,
    peer_sems,
    table_sems,
    kv_peer_sems,
    local_sems,
):
    g = lax.axis_index("groups")
    me = lax.axis_index("ctx")
    chips = n // 2
    half = chips // 2
    chip, core = me // 2, me % 2
    depth, width = weight_ref.shape[0], weights.shape[1]
    tok_rows = hidden_ref.shape[0]
    span = tok_rows // 2
    cut = depth // 2

    if chips > 8:
        spot = chip
    else:
        spot = (1 - chip % 2) * (chip // 2) + (chip % 2) * (chips - 1 - chip // 2)

    def index(position, which):
        p = (position + chips) % chips
        if chips > 8:
            return p * 2 + which
        back = p // half
        return 2 * ((1 - back) * 2 * p + back * (2 * (chips - 1 - p) + 1)) + which

    sibling = (g, chip * 2 + 1 - core)
    ring = ((g, index(spot + 1, core)), (g, index(spot - 1, core)))
    peers = [((g + d) % groups, me) for d in range(1, groups)]

    barrier = pltpu.get_barrier_semaphore()
    for device in (sibling, *ring, *peers):
        pl.semaphore_signal(barrier, inc=1, device_id=device, device_id_type=MESH)
    pl.semaphore_wait(barrier, 3 + len(peers))

    started = []

    def copy(source, target, send, receive, device):
        return pltpu.make_async_remote_copy(
            src_ref=source,
            dst_ref=target,
            send_sem=send,
            recv_sem=receive,
            device_id=device,
            device_id_type=MESH,
        )

    def send(*args):
        c = copy(*args)
        c.start()
        started.append(c)

    def gather(place, first, pieces, ready, ring_sems, across, own, between):
        def used(d, k, i):
            if k < half - 1:
                return True
            return (i < pieces // 2) == (d == 0)

        for i in range(pieces):
            ready(i)
            for d in range(2):
                if used(d, 0, i):
                    send(
                        first(i), place(me, i), ring_sems.at[0, d, 0, i],
                        ring_sems.at[1, d, 0, i], ring[d],
                    )
            send(first(i), place(me, i), own.at[0, i], own.at[1, i], sibling)
        between()
        for k in range(1, half + 1):
            for i in range(pieces):
                for d in range(2):
                    if not used(d, k - 1, i):
                        continue
                    at = place(index(spot - k if d == 0 else spot + k, core), i)
                    s, r = ring_sems.at[0, d, k - 1, i], ring_sems.at[1, d, k - 1, i]
                    copy(at, at, s, r, ring[d]).wait_recv()
                    if k < half and used(d, k, i):
                        send(at, at, ring_sems.at[0, d, k, i], ring_sems.at[1, d, k, i], ring[d])
                    send(at, at, across.at[0, d, k - 1, i], across.at[1, d, k - 1, i], sibling)
        for i in range(pieces):
            at = place(sibling[1], i)
            copy(at, at, own.at[0, i], own.at[1, i], sibling).wait_recv()
        for k in range(1, half + 1):
            for i in range(pieces):
                for d in range(2):
                    if used(d, k - 1, i):
                        at = place(index(spot - k if d == 0 else spot + k, 1 - core), i)
                        s, r = across.at[0, d, k - 1, i], across.at[1, d, k - 1, i]
                        copy(at, at, s, r, sibling).wait_recv()

    columns = pl.ds(pl.multiple_of(g * width, width), width)

    def weight_place(slot, i):
        return weights.at[pl.ds(pl.multiple_of(slot * depth + i * cut, cut), cut), :]

    locals_ = [
        pltpu.make_async_copy(
            weight_ref.at[:, columns],
            weights.at[pl.ds(pl.multiple_of(me * depth, depth), depth), :],
            local_sems.at[0],
        ),
        pltpu.make_async_copy(hidden_ref, states.at[g], local_sems.at[1]),
        pltpu.make_async_copy(queries_ref, asked, local_sems.at[2]),
    ]

    def between():
        for d, device in enumerate(peers):
            send(hidden_ref, states.at[g], peer_sems.at[0, d], peer_sems.at[1, d], device)
        for c in locals_:
            c.start()
        low = spans_ref[me]
        line = lax.broadcasted_iota(jnp.int32, (tok_rows, HD), 0)
        place = jnp.where(line < span, low * span, (2 * n - 2 - low) * span) + line
        angles = place.astype(jnp.float32) * frequency_ref[...]
        lane = lax.broadcasted_iota(jnp.int32, (tok_rows, HD), 1)
        sine = jnp.sin(angles)
        tables[g, 0] = jnp.cos(angles)
        tables[g, 1] = jnp.where(lane < HD // 2, -sine, sine)
        for d, device in enumerate(peers):
            send(
                tables.at[g], tables.at[g], table_sems.at[0, d], table_sems.at[1, d], device
            )
        for c in locals_:
            c.wait()

        def rotate(h, carry):
            x = asked[:, pl.ds(pl.multiple_of(h * HD, HD), HD)].astype(jnp.float32)
            y = x * tables[g, 0] + pltpu.roll(x, HD // 2, 1) * tables[g, 1]
            y = y.astype(jnp.bfloat16)
            rot_ref[0, h] = y[:span]
            rot_ref[1, h] = y[span:]
            return carry

        lax.fori_loop(0, QH, rotate, 0)

    gather(
        weight_place,
        lambda i: weight_ref.at[pl.ds(i * cut, cut), columns],
        2,
        lambda i: None,
        sems,
        side_sems,
        own_sems,
        between,
    )
    for d in range(groups - 1):
        source = (g + groups - 1 - d) % groups
        copy(
            states.at[source], states.at[source], peer_sems.at[0, d], peer_sems.at[1, d], peers[d]
        ).wait_recv()
        copy(
            tables.at[source], tables.at[source], table_sems.at[0, d], table_sems.at[1, d], peers[d]
        ).wait_recv()

    product[...] = jnp.zeros_like(product)

    def multiply(k, carry):
        at = pl.ds(pl.multiple_of(k * KBLOCK, KBLOCK), KBLOCK)
        x = states[:, :, at].reshape(groups * tok_rows, KBLOCK)
        product[...] += jnp.dot(
            x, weights[at, :], preferred_element_type=jnp.float32
        ).reshape(product.shape)
        return carry

    lax.fori_loop(0, states.shape[2] // KBLOCK, multiply, 0)

    is_key = g * width < KVH * HD

    def finish(which, store):
        for h in range(width // HD):
            x = product[which, :, h * HD : (h + 1) * HD]
            y = x * tables[which, 0] + pltpu.roll(x, HD // 2, 1) * tables[which, 1]
            store(h, jnp.where(is_key, y, x).astype(jnp.bfloat16))

    def store_own(h, value):
        kv_ref[g, me, :, h * HD : (h + 1) * HD] = value

    finish(g, store_own)

    def share():
        for d, device in enumerate(peers):

            def store(h, value, d=d):
                outgoing[d, :, h * HD : (h + 1) * HD] = value

            finish(device[0], store)
            send(
                outgoing.at[d], kv_ref.at[g, me], kv_peer_sems.at[0, d], kv_peer_sems.at[1, d],
                device,
            )

    def kv_place(slot, i):
        return kv_ref.at[(g + i) % groups, slot]

    def ready(i):
        if i == 1:
            share()
        if i:
            at = kv_place(me, i)
            d = groups - i - 1
            copy(at, at, kv_peer_sems.at[0, d], kv_peer_sems.at[1, d], peers[d]).wait_recv()

    gather(
        kv_place,
        lambda i: kv_place(me, i),
        groups,
        ready,
        kv_sems,
        kv_side_sems,
        kv_own_sems,
        lambda: None,
    )
    for c in started:
        c.wait_send()


def project(n, groups, weight, hidden, queries, span_pairs):
    depth, width = weight.shape[0], weight.shape[1] // groups
    tok_rows, wide = hidden.shape
    half = n // 4
    half_ids = jnp.arange(HD // 2, dtype=jnp.float32)
    frequency = ROPE_BASE ** (-(half_ids * 2.0 / HD))
    frequency = jnp.concatenate([frequency, frequency])[None]
    hbm = pl.BlockSpec(memory_space=pltpu.HBM)
    smem = pl.BlockSpec(memory_space=pltpu.SMEM)
    vmem = pl.BlockSpec(memory_space=pltpu.VMEM)
    dma = pltpu.SemaphoreType.DMA
    return pl.pallas_call(
        functools.partial(project_kernel, n, groups),
        out_shape=(
            jax.ShapeDtypeStruct((2, QH, tok_rows // 2, HD), jnp.bfloat16),
            jax.ShapeDtypeStruct((groups, n, tok_rows, width), jnp.bfloat16),
        ),
        in_specs=[hbm, hbm, hbm, smem, vmem],
        out_specs=(vmem, vmem),
        scratch_shapes=[
            pltpu.VMEM((n * depth, width), jnp.bfloat16),
            pltpu.VMEM((groups, tok_rows, wide), jnp.bfloat16),
            pltpu.VMEM(queries.shape, jnp.bfloat16),
            pltpu.VMEM((groups, 2, tok_rows, HD), jnp.float32),
            pltpu.VMEM((groups, tok_rows, width), jnp.float32),
            pltpu.VMEM((groups - 1, tok_rows, width), jnp.bfloat16),
            dma((2, 2, half, 2)),
            dma((2, 2, half, groups)),
            dma((2, 2, half, 2)),
            dma((2, 2, half, groups)),
            dma((2, 2)),
            dma((2, groups)),
            dma((2, groups - 1)),
            dma((2, groups - 1)),
            dma((2, groups - 1)),
            dma((3,)),
        ],
        compiler_params=pltpu.CompilerParams(
            collective_id=0, has_side_effects=True, vmem_limit_bytes=24 * 1024 * 1024
        ),
    )(weight, hidden, queries, span_pairs, frequency)


def body(groups, hidden, queries, cache_weight, pattern, span_pairs):
    tok_rows = hidden.shape[0]
    n = lax.axis_size("ctx")
    rotated, kv = project(n, groups, cache_weight, hidden, queries, span_pairs)
    kv = kv.reshape(groups, n * tok_rows, kv.shape[3])
    return attend(n, pattern, span_pairs, rotated, kv, tok_rows)


def solution(mesh):
    in_specs = (
        P(("groups", "ctx"), None),
        P(("groups", "ctx"), None),
        P("ctx", None),
        P("groups", None),
        P("groups"),
    )
    return jax.shard_map(
        functools.partial(body, mesh.shape["groups"]),
        mesh=mesh,
        in_specs=in_specs,
        out_specs=P(("groups", "ctx"), None),
        check_vma=False,
    )
```

```python
import functools
import math

import jax
import jax.numpy as jnp
from jax import lax
from jax.experimental import pallas as pl
from jax.experimental.pallas import tpu as pltpu
from jax.sharding import PartitionSpec as P

QH = 32
KVH = 4
HD = 128
BLOCK = 128
ROPE_BASE = 500000.0
MASKED = -1e30
CHUNK = 2 * BLOCK


def attend_long(part, count, chunks, offset, span, group, rot_ref, kbuf, vbuf, scores, out_ref):
    rows = group * span
    factor = HD ** (-0.5) * math.log2(math.e)
    for h in range(KVH):
        query = rot_ref[part, h * group : (h + 1) * group].reshape(rows, HD)

        def score(c, peak):
            keys = kbuf[h, pl.ds(pl.multiple_of(c * CHUNK, CHUNK), CHUNK), :]
            s = lax.dot_general(
                query, keys, (((1,), (1,)), ((), ())), preferred_element_type=jnp.float32
            )
            col = c * CHUNK + lax.broadcasted_iota(jnp.int32, (span, CHUNK), 1)
            line = offset + lax.broadcasted_iota(jnp.int32, (span, CHUNK), 0)
            live = (col < count * BLOCK) & ((col >= BLOCK) | (col <= line))
            bias = jnp.where(live, 0.0, MASKED)
            s = (s.reshape(group, span, CHUNK) + bias[None]).reshape(rows, CHUNK)
            scores[c] = s
            return jnp.maximum(peak, jnp.maximum(s[:, :BLOCK], s[:, BLOCK:]))

        peak = lax.fori_loop(
            0, chunks, score, jnp.full((rows, BLOCK), MASKED, jnp.float32)
        )
        top = jnp.max(peak, axis=1, keepdims=True)

        def mix(c, total):
            weights = jnp.exp2((scores[c] - top) * factor).astype(jnp.bfloat16)
            values = vbuf[h, pl.ds(pl.multiple_of(c * CHUNK, CHUNK), CHUNK), :]
            return total + jnp.dot(weights, values, preferred_element_type=jnp.float32)

        total = lax.fori_loop(0, chunks, mix, jnp.zeros((rows, 2 * HD), jnp.float32))
        result = (total[:, :HD] / total[:, HD:]).astype(jnp.bfloat16)
        for j in range(group):
            head = h * group + j
            out_ref[part * span : (part + 1) * span, head * HD : (head + 1) * HD] = result[
                j * span : (j + 1) * span
            ]


def attend_kernel(
    n, pattern_ref, spans_ref, rot_ref, kv_ref, out_ref, kbuf, vbuf, scores, owner
):
    me = lax.axis_index("ctx")
    tok_rows = out_ref.shape[0]
    span = tok_rows // 2
    width = kv_ref.shape[2]
    group = QH // KVH
    rows = group * span
    slots = pattern_ref.shape[1]
    factor = HD ** (-0.5) * math.log2(math.e)

    def place(d, carry):
        owner[spans_ref[d]] = d
        return carry

    lax.fori_loop(0, n, place, 0)
    vbuf[:, :, HD:] = jnp.ones_like(vbuf[:, :, HD:])
    low = spans_ref[me]

    for part in range(2):
        span_id = low if part == 0 else 2 * n - 1 - low
        query_block = span_id * span // BLOCK
        offset = span_id * span - query_block * BLOCK

        def fill(i, count):
            block = pattern_ref[query_block, i]

            @pl.when(block >= 0)
            def _():
                for e in range(2):
                    unit = 2 * block + e
                    upper = unit >= n
                    device = owner[jnp.where(upper, 2 * n - 1 - unit, unit)]
                    row = pl.multiple_of(device * tok_rows + jnp.where(upper, span, 0), span)
                    to = pl.ds(pl.multiple_of(count * BLOCK + e * span, span), span)
                    for h in range(KVH):
                        for buf, col in ((kbuf, h * HD), (vbuf, (KVH + h) * HD)):
                            buf[h, to, :HD] = kv_ref[
                                col // width, pl.ds(row, span), col % width : col % width + HD
                            ]

            return count + (block >= 0).astype(jnp.int32)

        count = lax.fori_loop(0, slots, fill, jnp.int32(0))

        @pl.when(count % 2 == 1)
        def _():
            to = pl.ds(pl.multiple_of(count * BLOCK, BLOCK), BLOCK)
            kbuf[:, to, :] = jnp.zeros((KVH, BLOCK, HD), kbuf.dtype)
            vbuf[:, to, :HD] = jnp.zeros((KVH, BLOCK, HD), vbuf.dtype)

        chunks = (count + 1) // 2

        if scores.shape[0] > 4:
            attend_long(
                part, count, chunks, offset, span, group, rot_ref, kbuf, vbuf, scores, out_ref
            )
            continue

        line = offset + lax.broadcasted_iota(jnp.int32, (span, BLOCK), 0)
        col = lax.broadcasted_iota(jnp.int32, (span, BLOCK), 1)
        first_bias = jnp.where(col <= line, 0.0, MASKED)[None]
        last_bias = jnp.where(count % 2 == 1, MASKED, 0.0)

        for v in range(1, scores.shape[0] + 1):

            @pl.when(chunks == v)
            def _(v=v):
                def one_head(h, carry):
                    query = rot_ref[part, pl.ds(h * group, group)].reshape(rows, HD)
                    keys = kbuf[h, : v * CHUNK]
                    s = lax.dot_general(
                        query, keys, (((1,), (1,)), ((), ())), preferred_element_type=jnp.float32
                    )
                    front = s[:, :BLOCK].reshape(group, span, BLOCK) + first_bias
                    pieces = [front.reshape(rows, BLOCK)]
                    if v > 1:
                        pieces.append(s[:, BLOCK:-BLOCK])
                    pieces.append(s[:, -BLOCK:] + last_bias)
                    s = jnp.concatenate(pieces, axis=1)
                    top = jnp.max(s, axis=1, keepdims=True)
                    weights = jnp.exp2((s - top) * factor).astype(jnp.bfloat16)
                    total = jnp.dot(
                        weights, vbuf[h, : v * CHUNK], preferred_element_type=jnp.float32
                    )
                    result = (total[:, :HD] / total[:, HD:]).astype(jnp.bfloat16)
                    for j in range(group):
                        to = pl.ds(pl.multiple_of((h * group + j) * HD, HD), HD)
                        out_ref[part * span : (part + 1) * span, to] = result[
                            j * span : (j + 1) * span
                        ]
                    return carry

                lax.fori_loop(0, KVH, one_head, 0)


def attend(n, pattern, span_pairs, rotated, kv, tok_rows):
    span = tok_rows // 2
    chunks = (pattern.shape[1] + 1) // 2
    keys = chunks * CHUNK
    rows = QH // KVH * span
    smem = pl.BlockSpec(memory_space=pltpu.SMEM)
    vmem = pl.BlockSpec(memory_space=pltpu.VMEM)
    return pl.pallas_call(
        functools.partial(attend_kernel, n),
        out_shape=jax.ShapeDtypeStruct((tok_rows, QH * HD), jnp.bfloat16),
        in_specs=[smem, smem, vmem, vmem],
        out_specs=vmem,
        scratch_shapes=[
            pltpu.VMEM((KVH, keys, HD), jnp.bfloat16),
            pltpu.VMEM((KVH, keys, 2 * HD), jnp.bfloat16),
            pltpu.VMEM((chunks, rows, CHUNK), jnp.float32),
            pltpu.SMEM((n,), jnp.int32),
        ],
        compiler_params=pltpu.CompilerParams(vmem_limit_bytes=24 * 1024 * 1024),
    )(pattern, span_pairs, rotated, kv)


MESH = pl.DeviceIdType.MESH
KBLOCK = 512


def project_kernel(
    n,
    groups,
    weight_ref,
    hidden_ref,
    queries_ref,
    spans_ref,
    frequency_ref,
    rot_ref,
    kv_ref,
    weights,
    states,
    asked,
    tables,
    product,
    outgoing,
    sems,
    kv_sems,
    side_sems,
    kv_side_sems,
    own_sems,
    kv_own_sems,
    peer_sems,
    table_sems,
    kv_peer_sems,
    local_sems,
):
    g = lax.axis_index("groups")
    me = lax.axis_index("ctx")
    chips = n // 2
    half = chips // 2
    chip, core = me // 2, me % 2
    depth, width = weight_ref.shape[0], weights.shape[1]
    tok_rows = hidden_ref.shape[0]
    span = tok_rows // 2
    cut = depth // 2

    if chips > 8:
        spot = chip
    else:
        spot = (1 - chip % 2) * (chip // 2) + (chip % 2) * (chips - 1 - chip // 2)

    def index(position, which):
        p = (position + chips) % chips
        if chips > 8:
            return p * 2 + which
        back = p // half
        return 2 * ((1 - back) * 2 * p + back * (2 * (chips - 1 - p) + 1)) + which

    sibling = (g, chip * 2 + 1 - core)
    ring = ((g, index(spot + 1, core)), (g, index(spot - 1, core)))
    peers = [((g + d) % groups, me) for d in range(1, groups)]

    barrier = pltpu.get_barrier_semaphore()
    for device in (sibling, *ring, *peers):
        pl.semaphore_signal(barrier, inc=1, device_id=device, device_id_type=MESH)
    pl.semaphore_wait(barrier, 3 + len(peers))

    started = []

    def copy(source, target, send, receive, device):
        return pltpu.make_async_remote_copy(
            src_ref=source,
            dst_ref=target,
            send_sem=send,
            recv_sem=receive,
            device_id=device,
            device_id_type=MESH,
        )

    def send(*args):
        c = copy(*args)
        c.start()
        started.append(c)

    def gather(place, first, pieces, ready, ring_sems, across, own, between):
        def used(d, k, i):
            if k < half - 1:
                return True
            return (i < pieces // 2) == (d == 0)

        for i in range(pieces):
            ready(i)
            for d in range(2):
                if used(d, 0, i):
                    send(
                        first(i), place(me, i), ring_sems.at[0, d, 0, i],
                        ring_sems.at[1, d, 0, i], ring[d],
                    )
            send(first(i), place(me, i), own.at[0, i], own.at[1, i], sibling)
        between()
        for k in range(1, half + 1):
            for i in range(pieces):
                for d in range(2):
                    if not used(d, k - 1, i):
                        continue
                    at = place(index(spot - k if d == 0 else spot + k, core), i)
                    s, r = ring_sems.at[0, d, k - 1, i], ring_sems.at[1, d, k - 1, i]
                    copy(at, at, s, r, ring[d]).wait_recv()
                    if k < half and used(d, k, i):
                        send(at, at, ring_sems.at[0, d, k, i], ring_sems.at[1, d, k, i], ring[d])
                    send(at, at, across.at[0, d, k - 1, i], across.at[1, d, k - 1, i], sibling)
        for i in range(pieces):
            at = place(sibling[1], i)
            copy(at, at, own.at[0, i], own.at[1, i], sibling).wait_recv()
        for k in range(1, half + 1):
            for i in range(pieces):
                for d in range(2):
                    if used(d, k - 1, i):
                        at = place(index(spot - k if d == 0 else spot + k, 1 - core), i)
                        s, r = across.at[0, d, k - 1, i], across.at[1, d, k - 1, i]
                        copy(at, at, s, r, sibling).wait_recv()

    columns = pl.ds(pl.multiple_of(g * width, width), width)

    def weight_place(slot, i):
        return weights.at[pl.ds(pl.multiple_of(slot * depth + i * cut, cut), cut), :]

    locals_ = [
        pltpu.make_async_copy(
            weight_ref.at[:, columns],
            weights.at[pl.ds(pl.multiple_of(me * depth, depth), depth), :],
            local_sems.at[0],
        ),
        pltpu.make_async_copy(hidden_ref, states.at[g], local_sems.at[1]),
        pltpu.make_async_copy(queries_ref, asked, local_sems.at[2]),
    ]

    def between():
        for d, device in enumerate(peers):
            send(hidden_ref, states.at[g], peer_sems.at[0, d], peer_sems.at[1, d], device)
        for c in locals_:
            c.start()
        low = spans_ref[me]
        line = lax.broadcasted_iota(jnp.int32, (tok_rows, HD), 0)
        place = jnp.where(line < span, low * span, (2 * n - 2 - low) * span) + line
        angles = place.astype(jnp.float32) * frequency_ref[...]
        lane = lax.broadcasted_iota(jnp.int32, (tok_rows, HD), 1)
        sine = jnp.sin(angles)
        tables[g, 0] = jnp.cos(angles)
        tables[g, 1] = jnp.where(lane < HD // 2, -sine, sine)
        for d, device in enumerate(peers):
            send(
                tables.at[g], tables.at[g], table_sems.at[0, d], table_sems.at[1, d], device
            )
        for c in locals_:
            c.wait()

        def rotate(h, carry):
            x = asked[:, pl.ds(pl.multiple_of(h * HD, HD), HD)].astype(jnp.float32)
            y = x * tables[g, 0] + pltpu.roll(x, HD // 2, 1) * tables[g, 1]
            y = y.astype(jnp.bfloat16)
            rot_ref[0, h] = y[:span]
            rot_ref[1, h] = y[span:]
            return carry

        lax.fori_loop(0, QH, rotate, 0)

    gather(
        weight_place,
        lambda i: weight_ref.at[pl.ds(i * cut, cut), columns],
        2,
        lambda i: None,
        sems,
        side_sems,
        own_sems,
        between,
    )
    for d in range(groups - 1):
        source = (g + groups - 1 - d) % groups
        copy(
            states.at[source], states.at[source], peer_sems.at[0, d], peer_sems.at[1, d], peers[d]
        ).wait_recv()
        copy(
            tables.at[source], tables.at[source], table_sems.at[0, d], table_sems.at[1, d], peers[d]
        ).wait_recv()

    product[...] = jnp.zeros_like(product)

    def multiply(k, carry):
        at = pl.ds(pl.multiple_of(k * KBLOCK, KBLOCK), KBLOCK)
        x = states[:, :, at].reshape(groups * tok_rows, KBLOCK)
        product[...] += jnp.dot(
            x, weights[at, :], preferred_element_type=jnp.float32
        ).reshape(product.shape)
        return carry

    lax.fori_loop(0, states.shape[2] // KBLOCK, multiply, 0)

    is_key = g * width < KVH * HD

    def finish(which, store):
        for h in range(width // HD):
            x = product[which, :, h * HD : (h + 1) * HD]
            y = x * tables[which, 0] + pltpu.roll(x, HD // 2, 1) * tables[which, 1]
            store(h, jnp.where(is_key, y, x).astype(jnp.bfloat16))

    def store_own(h, value):
        kv_ref[g, me, :, h * HD : (h + 1) * HD] = value

    finish(g, store_own)

    def share():
        for d, device in enumerate(peers):

            def store(h, value, d=d):
                outgoing[d, :, h * HD : (h + 1) * HD] = value

            finish(device[0], store)
            send(
                outgoing.at[d], kv_ref.at[g, me], kv_peer_sems.at[0, d], kv_peer_sems.at[1, d],
                device,
            )

    def kv_place(slot, i):
        return kv_ref.at[(g + i) % groups, slot]

    def ready(i):
        if i == 1:
            share()
        if i:
            at = kv_place(me, i)
            d = groups - i - 1
            copy(at, at, kv_peer_sems.at[0, d], kv_peer_sems.at[1, d], peers[d]).wait_recv()

    gather(
        kv_place,
        lambda i: kv_place(me, i),
        groups,
        ready,
        kv_sems,
        kv_side_sems,
        kv_own_sems,
        lambda: None,
    )
    for c in started:
        c.wait_send()


def project(n, groups, weight, hidden, queries, span_pairs):
    depth, width = weight.shape[0], weight.shape[1] // groups
    tok_rows, wide = hidden.shape
    half = n // 4
    half_ids = jnp.arange(HD // 2, dtype=jnp.float32)
    frequency = ROPE_BASE ** (-(half_ids * 2.0 / HD))
    frequency = jnp.concatenate([frequency, frequency])[None]
    hbm = pl.BlockSpec(memory_space=pltpu.HBM)
    smem = pl.BlockSpec(memory_space=pltpu.SMEM)
    vmem = pl.BlockSpec(memory_space=pltpu.VMEM)
    dma = pltpu.SemaphoreType.DMA
    return pl.pallas_call(
        functools.partial(project_kernel, n, groups),
        out_shape=(
            jax.ShapeDtypeStruct((2, QH, tok_rows // 2, HD), jnp.bfloat16),
            jax.ShapeDtypeStruct((groups, n, tok_rows, width), jnp.bfloat16),
        ),
        in_specs=[hbm, hbm, hbm, smem, vmem],
        out_specs=(vmem, vmem),
        scratch_shapes=[
            pltpu.VMEM((n * depth, width), jnp.bfloat16),
            pltpu.VMEM((groups, tok_rows, wide), jnp.bfloat16),
            pltpu.VMEM(queries.shape, jnp.bfloat16),
            pltpu.VMEM((groups, 2, tok_rows, HD), jnp.float32),
            pltpu.VMEM((groups, tok_rows, width), jnp.float32),
            pltpu.VMEM((groups - 1, tok_rows, width), jnp.bfloat16),
            dma((2, 2, half, 2)),
            dma((2, 2, half, groups)),
            dma((2, 2, half, 2)),
            dma((2, 2, half, groups)),
            dma((2, 2)),
            dma((2, groups)),
            dma((2, groups - 1)),
            dma((2, groups - 1)),
            dma((2, groups - 1)),
            dma((3,)),
        ],
        compiler_params=pltpu.CompilerParams(
            collective_id=0, has_side_effects=True, vmem_limit_bytes=24 * 1024 * 1024
        ),
    )(weight, hidden, queries, span_pairs, frequency)


def body(groups, hidden, queries, cache_weight, pattern, span_pairs):
    tok_rows = hidden.shape[0]
    n = lax.axis_size("ctx")
    rotated, kv = project(n, groups, cache_weight, hidden, queries, span_pairs)
    kv = kv.reshape(groups, n * tok_rows, kv.shape[3])
    return attend(n, pattern, span_pairs, rotated, kv, tok_rows)


def solution(mesh):
    in_specs = (
        P(("groups", "ctx"), None),
        P(("groups", "ctx"), None),
        P("ctx", None),
        P("groups", None),
        P("groups"),
    )
    return jax.shard_map(
        functools.partial(body, mesh.shape["groups"]),
        mesh=mesh,
        in_specs=in_specs,
        out_specs=P(("groups", "ctx"), None),
        check_vma=False,
    )
```

```python
import functools
import math

import jax
import jax.numpy as jnp
from jax import lax
from jax.experimental import pallas as pl
from jax.experimental.pallas import tpu as pltpu
from jax.sharding import PartitionSpec as P

QH = 32
KVH = 4
HD = 128
BLOCK = 128
ROPE_BASE = 500000.0
MASKED = -1e30
CHUNK = 2 * BLOCK


def attend_long(part, count, chunks, offset, span, group, rot_ref, kbuf, vbuf, scores, out_ref):
    rows = group * span
    factor = HD ** (-0.5) * math.log2(math.e)
    for h in range(KVH):
        query = rot_ref[part, h * group : (h + 1) * group].reshape(rows, HD)

        def score(c, peak):
            keys = kbuf[h, pl.ds(pl.multiple_of(c * CHUNK, CHUNK), CHUNK), :]
            s = lax.dot_general(
                query, keys, (((1,), (1,)), ((), ())), preferred_element_type=jnp.float32
            )
            col = c * CHUNK + lax.broadcasted_iota(jnp.int32, (span, CHUNK), 1)
            line = offset + lax.broadcasted_iota(jnp.int32, (span, CHUNK), 0)
            live = (col < count * BLOCK) & ((col >= BLOCK) | (col <= line))
            bias = jnp.where(live, 0.0, MASKED)
            s = (s.reshape(group, span, CHUNK) + bias[None]).reshape(rows, CHUNK)
            scores[c] = s
            return jnp.maximum(peak, jnp.maximum(s[:, :BLOCK], s[:, BLOCK:]))

        peak = lax.fori_loop(
            0, chunks, score, jnp.full((rows, BLOCK), MASKED, jnp.float32)
        )
        top = jnp.max(peak, axis=1, keepdims=True)

        def mix(c, total):
            weights = jnp.exp2((scores[c] - top) * factor).astype(jnp.bfloat16)
            values = vbuf[h, pl.ds(pl.multiple_of(c * CHUNK, CHUNK), CHUNK), :]
            return total + jnp.dot(weights, values, preferred_element_type=jnp.float32)

        total = lax.fori_loop(0, chunks, mix, jnp.zeros((rows, 2 * HD), jnp.float32))
        result = (total[:, :HD] / total[:, HD:]).astype(jnp.bfloat16)
        for j in range(group):
            head = h * group + j
            out_ref[part * span : (part + 1) * span, head * HD : (head + 1) * HD] = result[
                j * span : (j + 1) * span
            ]


def attend_kernel(
    n, pattern_ref, spans_ref, rot_ref, kv_ref, out_ref, kbuf, vbuf, scores, owner
):
    me = lax.axis_index("ctx")
    tok_rows = out_ref.shape[0]
    span = tok_rows // 2
    width = kv_ref.shape[2]
    group = QH // KVH
    rows = group * span
    slots = pattern_ref.shape[1]
    factor = HD ** (-0.5) * math.log2(math.e)

    def place(d, carry):
        owner[spans_ref[d]] = d
        return carry

    lax.fori_loop(0, n, place, 0)
    vbuf[:, :, HD:] = jnp.ones_like(vbuf[:, :, HD:])
    low = spans_ref[me]

    for part in range(2):
        span_id = low if part == 0 else 2 * n - 1 - low
        query_block = span_id * span // BLOCK
        offset = span_id * span - query_block * BLOCK

        def fill(i, count):
            block = pattern_ref[query_block, i]

            @pl.when(block >= 0)
            def _():
                for e in range(2):
                    unit = 2 * block + e
                    upper = unit >= n
                    device = owner[jnp.where(upper, 2 * n - 1 - unit, unit)]
                    row = pl.multiple_of(device * tok_rows + jnp.where(upper, span, 0), span)
                    to = pl.ds(pl.multiple_of(count * BLOCK + e * span, span), span)
                    for h in range(KVH):
                        for buf, col in ((kbuf, h * HD), (vbuf, (KVH + h) * HD)):
                            buf[h, to, :HD] = kv_ref[
                                col // width, pl.ds(row, span), col % width : col % width + HD
                            ]

            return count + (block >= 0).astype(jnp.int32)

        count = lax.fori_loop(0, slots, fill, jnp.int32(0))

        @pl.when(count % 2 == 1)
        def _():
            to = pl.ds(pl.multiple_of(count * BLOCK, BLOCK), BLOCK)
            kbuf[:, to, :] = jnp.zeros((KVH, BLOCK, HD), kbuf.dtype)
            vbuf[:, to, :HD] = jnp.zeros((KVH, BLOCK, HD), vbuf.dtype)

        chunks = (count + 1) // 2

        if scores.shape[0] > 4:
            attend_long(
                part, count, chunks, offset, span, group, rot_ref, kbuf, vbuf, scores, out_ref
            )
            continue

        line = offset + lax.broadcasted_iota(jnp.int32, (span, BLOCK), 0)
        col = lax.broadcasted_iota(jnp.int32, (span, BLOCK), 1)
        first_bias = jnp.where(col <= line, 0.0, MASKED)[None]
        last_bias = jnp.where(count % 2 == 1, MASKED, 0.0)

        for v in range(1, scores.shape[0] + 1):

            @pl.when(chunks == v)
            def _(v=v):
                def one_head(h, carry):
                    query = rot_ref[part, pl.ds(h * group, group)].reshape(rows, HD)
                    keys = kbuf[h, : v * CHUNK]
                    s = lax.dot_general(
                        query, keys, (((1,), (1,)), ((), ())), preferred_element_type=jnp.float32
                    )
                    front = s[:, :BLOCK].reshape(group, span, BLOCK) + first_bias
                    pieces = [front.reshape(rows, BLOCK)]
                    if v > 1:
                        pieces.append(s[:, BLOCK:-BLOCK])
                    pieces.append(s[:, -BLOCK:] + last_bias)
                    s = jnp.concatenate(pieces, axis=1)
                    top = jnp.max(s, axis=1, keepdims=True)
                    weights = jnp.exp2((s - top) * factor).astype(jnp.bfloat16)
                    total = jnp.dot(
                        weights, vbuf[h, : v * CHUNK], preferred_element_type=jnp.float32
                    )
                    result = (total[:, :HD] / total[:, HD:]).astype(jnp.bfloat16)
                    for j in range(group):
                        to = pl.ds(pl.multiple_of((h * group + j) * HD, HD), HD)
                        out_ref[part * span : (part + 1) * span, to] = result[
                            j * span : (j + 1) * span
                        ]
                    return carry

                lax.fori_loop(0, KVH, one_head, 0)


def attend(n, pattern, span_pairs, rotated, kv, tok_rows):
    span = tok_rows // 2
    chunks = (pattern.shape[1] + 1) // 2
    keys = chunks * CHUNK
    rows = QH // KVH * span
    smem = pl.BlockSpec(memory_space=pltpu.SMEM)
    vmem = pl.BlockSpec(memory_space=pltpu.VMEM)
    return pl.pallas_call(
        functools.partial(attend_kernel, n),
        out_shape=jax.ShapeDtypeStruct((tok_rows, QH * HD), jnp.bfloat16),
        in_specs=[smem, smem, vmem, vmem],
        out_specs=vmem,
        scratch_shapes=[
            pltpu.VMEM((KVH, keys, HD), jnp.bfloat16),
            pltpu.VMEM((KVH, keys, 2 * HD), jnp.bfloat16),
            pltpu.VMEM((chunks, rows, CHUNK), jnp.float32),
            pltpu.SMEM((n,), jnp.int32),
        ],
        compiler_params=pltpu.CompilerParams(vmem_limit_bytes=24 * 1024 * 1024),
    )(pattern, span_pairs, rotated, kv)


MESH = pl.DeviceIdType.MESH
KBLOCK = 512


def project_kernel(
    n,
    groups,
    weight_ref,
    hidden_ref,
    queries_ref,
    spans_ref,
    frequency_ref,
    rot_ref,
    kv_ref,
    weights,
    states,
    asked,
    tables,
    product,
    outgoing,
    sems,
    kv_sems,
    side_sems,
    kv_side_sems,
    own_sems,
    kv_own_sems,
    peer_sems,
    table_sems,
    kv_peer_sems,
    local_sems,
):
    g = lax.axis_index("groups")
    me = lax.axis_index("ctx")
    chips = n // 2
    half = chips // 2
    chip, core = me // 2, me % 2
    depth, width = weight_ref.shape[0], weights.shape[1]
    tok_rows = hidden_ref.shape[0]
    span = tok_rows // 2
    cut = depth // 2

    if chips > 8:
        spot = chip
    else:
        spot = (1 - chip % 2) * (chip // 2) + (chip % 2) * (chips - 1 - chip // 2)

    def index(position, which):
        p = (position + chips) % chips
        if chips > 8:
            return p * 2 + which
        back = p // half
        return 2 * ((1 - back) * 2 * p + back * (2 * (chips - 1 - p) + 1)) + which

    sibling = (g, chip * 2 + 1 - core)
    ring = ((g, index(spot + 1, core)), (g, index(spot - 1, core)))
    peers = [((g + d) % groups, me) for d in range(1, groups)]

    barrier = pltpu.get_barrier_semaphore()
    for device in (sibling, *ring, *peers):
        pl.semaphore_signal(barrier, inc=1, device_id=device, device_id_type=MESH)
    pl.semaphore_wait(barrier, 3 + len(peers))

    started = []

    def copy(source, target, send, receive, device):
        return pltpu.make_async_remote_copy(
            src_ref=source,
            dst_ref=target,
            send_sem=send,
            recv_sem=receive,
            device_id=device,
            device_id_type=MESH,
        )

    def send(*args):
        c = copy(*args)
        c.start()
        started.append(c)

    def gather(place, first, pieces, ready, ring_sems, across, own, between):
        def used(d, k, i):
            if k < half - 1:
                return True
            return (i < pieces // 2) == (d == 0)

        for i in range(pieces):
            ready(i)
            for d in range(2):
                if used(d, 0, i):
                    send(
                        first(i), place(me, i), ring_sems.at[0, d, 0, i],
                        ring_sems.at[1, d, 0, i], ring[d],
                    )
            send(first(i), place(me, i), own.at[0, i], own.at[1, i], sibling)
        between()
        for k in range(1, half + 1):
            for i in range(pieces):
                for d in range(2):
                    if not used(d, k - 1, i):
                        continue
                    at = place(index(spot - k if d == 0 else spot + k, core), i)
                    s, r = ring_sems.at[0, d, k - 1, i], ring_sems.at[1, d, k - 1, i]
                    copy(at, at, s, r, ring[d]).wait_recv()
                    if k < half and used(d, k, i):
                        send(at, at, ring_sems.at[0, d, k, i], ring_sems.at[1, d, k, i], ring[d])
                    send(at, at, across.at[0, d, k - 1, i], across.at[1, d, k - 1, i], sibling)
        for i in range(pieces):
            at = place(sibling[1], i)
            copy(at, at, own.at[0, i], own.at[1, i], sibling).wait_recv()
        for k in range(1, half + 1):
            for i in range(pieces):
                for d in range(2):
                    if used(d, k - 1, i):
                        at = place(index(spot - k if d == 0 else spot + k, 1 - core), i)
                        s, r = across.at[0, d, k - 1, i], across.at[1, d, k - 1, i]
                        copy(at, at, s, r, sibling).wait_recv()

    columns = pl.ds(pl.multiple_of(g * width, width), width)

    def weight_place(slot, i):
        return weights.at[pl.ds(pl.multiple_of(slot * depth + i * cut, cut), cut), :]

    locals_ = [
        pltpu.make_async_copy(
            weight_ref.at[:, columns],
            weights.at[pl.ds(pl.multiple_of(me * depth, depth), depth), :],
            local_sems.at[0],
        ),
        pltpu.make_async_copy(hidden_ref, states.at[g], local_sems.at[1]),
        pltpu.make_async_copy(queries_ref, asked, local_sems.at[2]),
    ]

    def between():
        for d, device in enumerate(peers):
            send(hidden_ref, states.at[g], peer_sems.at[0, d], peer_sems.at[1, d], device)
        for c in locals_:
            c.start()
        low = spans_ref[me]
        line = lax.broadcasted_iota(jnp.int32, (tok_rows, HD), 0)
        place = jnp.where(line < span, low * span, (2 * n - 2 - low) * span) + line
        angles = place.astype(jnp.float32) * frequency_ref[...]
        lane = lax.broadcasted_iota(jnp.int32, (tok_rows, HD), 1)
        sine = jnp.sin(angles)
        tables[g, 0] = jnp.cos(angles)
        tables[g, 1] = jnp.where(lane < HD // 2, -sine, sine)
        for d, device in enumerate(peers):
            send(
                tables.at[g], tables.at[g], table_sems.at[0, d], table_sems.at[1, d], device
            )
        for c in locals_:
            c.wait()

        def rotate(h, carry):
            x = asked[:, pl.ds(pl.multiple_of(h * HD, HD), HD)].astype(jnp.float32)
            y = x * tables[g, 0] + pltpu.roll(x, HD // 2, 1) * tables[g, 1]
            y = y.astype(jnp.bfloat16)
            rot_ref[0, h] = y[:span]
            rot_ref[1, h] = y[span:]
            return carry

        lax.fori_loop(0, QH, rotate, 0)

    gather(
        weight_place,
        lambda i: weight_ref.at[pl.ds(i * cut, cut), columns],
        2,
        lambda i: None,
        sems,
        side_sems,
        own_sems,
        between,
    )
    for d in range(groups - 1):
        source = (g + groups - 1 - d) % groups
        copy(
            states.at[source], states.at[source], peer_sems.at[0, d], peer_sems.at[1, d], peers[d]
        ).wait_recv()
        copy(
            tables.at[source], tables.at[source], table_sems.at[0, d], table_sems.at[1, d], peers[d]
        ).wait_recv()

    product[...] = jnp.zeros_like(product)

    def multiply(k, carry):
        at = pl.ds(pl.multiple_of(k * KBLOCK, KBLOCK), KBLOCK)
        x = states[:, :, at].reshape(groups * tok_rows, KBLOCK)
        product[...] += jnp.dot(
            x, weights[at, :], preferred_element_type=jnp.float32
        ).reshape(product.shape)
        return carry

    lax.fori_loop(0, states.shape[2] // KBLOCK, multiply, 0)

    is_key = g * width < KVH * HD

    def finish(which, store):
        for h in range(width // HD):
            x = product[which, :, h * HD : (h + 1) * HD]
            y = x * tables[which, 0] + pltpu.roll(x, HD // 2, 1) * tables[which, 1]
            store(h, jnp.where(is_key, y, x).astype(jnp.bfloat16))

    def store_own(h, value):
        kv_ref[g, me, :, h * HD : (h + 1) * HD] = value

    finish(g, store_own)

    def share():
        for d, device in enumerate(peers):

            def store(h, value, d=d):
                outgoing[d, :, h * HD : (h + 1) * HD] = value

            finish(device[0], store)
            send(
                outgoing.at[d], kv_ref.at[g, me], kv_peer_sems.at[0, d], kv_peer_sems.at[1, d],
                device,
            )

    def kv_place(slot, i):
        return kv_ref.at[(g + i) % groups, slot]

    def ready(i):
        if i == 1:
            share()
        if i:
            at = kv_place(me, i)
            d = groups - i - 1
            copy(at, at, kv_peer_sems.at[0, d], kv_peer_sems.at[1, d], peers[d]).wait_recv()

    gather(
        kv_place,
        lambda i: kv_place(me, i),
        groups,
        ready,
        kv_sems,
        kv_side_sems,
        kv_own_sems,
        lambda: None,
    )
    for c in started:
        c.wait_send()


def project(n, groups, weight, hidden, queries, span_pairs):
    depth, width = weight.shape[0], weight.shape[1] // groups
    tok_rows, wide = hidden.shape
    half = n // 4
    half_ids = jnp.arange(HD // 2, dtype=jnp.float32)
    frequency = ROPE_BASE ** (-(half_ids * 2.0 / HD))
    frequency = jnp.concatenate([frequency, frequency])[None]
    hbm = pl.BlockSpec(memory_space=pltpu.HBM)
    smem = pl.BlockSpec(memory_space=pltpu.SMEM)
    vmem = pl.BlockSpec(memory_space=pltpu.VMEM)
    dma = pltpu.SemaphoreType.DMA
    weight, hidden, queries = (
        pltpu.with_memory_space_constraint(x, pltpu.HBM) for x in (weight, hidden, queries)
    )
    return pl.pallas_call(
        functools.partial(project_kernel, n, groups),
        out_shape=(
            jax.ShapeDtypeStruct((2, QH, tok_rows // 2, HD), jnp.bfloat16),
            jax.ShapeDtypeStruct((groups, n, tok_rows, width), jnp.bfloat16),
        ),
        in_specs=[hbm, hbm, hbm, smem, vmem],
        out_specs=(vmem, vmem),
        scratch_shapes=[
            pltpu.VMEM((n * depth, width), jnp.bfloat16),
            pltpu.VMEM((groups, tok_rows, wide), jnp.bfloat16),
            pltpu.VMEM(queries.shape, jnp.bfloat16),
            pltpu.VMEM((groups, 2, tok_rows, HD), jnp.float32),
            pltpu.VMEM((groups, tok_rows, width), jnp.float32),
            pltpu.VMEM((groups - 1, tok_rows, width), jnp.bfloat16),
            dma((2, 2, half, 2)),
            dma((2, 2, half, groups)),
            dma((2, 2, half, 2)),
            dma((2, 2, half, groups)),
            dma((2, 2)),
            dma((2, groups)),
            dma((2, groups - 1)),
            dma((2, groups - 1)),
            dma((2, groups - 1)),
            dma((3,)),
        ],
        compiler_params=pltpu.CompilerParams(
            collective_id=0, has_side_effects=True, vmem_limit_bytes=24 * 1024 * 1024
        ),
    )(weight, hidden, queries, span_pairs, frequency)


def body(groups, hidden, queries, cache_weight, pattern, span_pairs):
    tok_rows = hidden.shape[0]
    n = lax.axis_size("ctx")
    rotated, kv = project(n, groups, cache_weight, hidden, queries, span_pairs)
    kv = kv.reshape(groups, n * tok_rows, kv.shape[3])
    return attend(n, pattern, span_pairs, rotated, kv, tok_rows)


def solution(mesh):
    in_specs = (
        P(("groups", "ctx"), None),
        P(("groups", "ctx"), None),
        P("ctx", None),
        P("groups", None),
        P("groups"),
    )
    return jax.shard_map(
        functools.partial(body, mesh.shape["groups"]),
        mesh=mesh,
        in_specs=in_specs,
        out_specs=P(("groups", "ctx"), None),
        check_vma=False,
    )
```

```python
import functools
import math

import jax
import jax.numpy as jnp
from jax import lax
from jax.experimental import pallas as pl
from jax.experimental.pallas import tpu as pltpu
from jax.sharding import PartitionSpec as P

QH = 32
KVH = 4
HD = 128
BLOCK = 128
ROPE_BASE = 500000.0
MASKED = -1e30
CHUNK = 2 * BLOCK


def attend_long(part, count, chunks, offset, span, group, rot_ref, kbuf, vbuf, scores, out_ref):
    rows = group * span
    factor = HD ** (-0.5) * math.log2(math.e)
    for h in range(KVH):
        query = rot_ref[part, h * group : (h + 1) * group].reshape(rows, HD)

        def score(c, peak):
            keys = kbuf[h, pl.ds(pl.multiple_of(c * CHUNK, CHUNK), CHUNK), :]
            s = lax.dot_general(
                query, keys, (((1,), (1,)), ((), ())), preferred_element_type=jnp.float32
            )
            col = c * CHUNK + lax.broadcasted_iota(jnp.int32, (span, CHUNK), 1)
            line = offset + lax.broadcasted_iota(jnp.int32, (span, CHUNK), 0)
            live = (col < count * BLOCK) & ((col >= BLOCK) | (col <= line))
            bias = jnp.where(live, 0.0, MASKED)
            s = (s.reshape(group, span, CHUNK) + bias[None]).reshape(rows, CHUNK)
            scores[c] = s
            return jnp.maximum(peak, jnp.maximum(s[:, :BLOCK], s[:, BLOCK:]))

        peak = lax.fori_loop(
            0, chunks, score, jnp.full((rows, BLOCK), MASKED, jnp.float32)
        )
        top = jnp.max(peak, axis=1, keepdims=True)

        def mix(c, total):
            weights = jnp.exp2((scores[c] - top) * factor).astype(jnp.bfloat16)
            values = vbuf[h, pl.ds(pl.multiple_of(c * CHUNK, CHUNK), CHUNK), :]
            return total + jnp.dot(weights, values, preferred_element_type=jnp.float32)

        total = lax.fori_loop(0, chunks, mix, jnp.zeros((rows, 2 * HD), jnp.float32))
        result = (total[:, :HD] / total[:, HD:]).astype(jnp.bfloat16)
        for j in range(group):
            head = h * group + j
            out_ref[part * span : (part + 1) * span, head * HD : (head + 1) * HD] = result[
                j * span : (j + 1) * span
            ]


def attend_kernel(
    n, pattern_ref, spans_ref, rot_ref, kv_ref, out_ref, kbuf, vbuf, scores, owner
):
    me = lax.axis_index("ctx")
    tok_rows = out_ref.shape[0]
    span = tok_rows // 2
    width = kv_ref.shape[2]
    group = QH // KVH
    rows = group * span
    slots = pattern_ref.shape[1]
    factor = HD ** (-0.5) * math.log2(math.e)

    def place(d, carry):
        owner[spans_ref[d]] = d
        return carry

    lax.fori_loop(0, n, place, 0)
    vbuf[:, :, HD:] = jnp.ones_like(vbuf[:, :, HD:])
    low = spans_ref[me]

    for part in range(2):
        span_id = low if part == 0 else 2 * n - 1 - low
        query_block = span_id * span // BLOCK
        offset = span_id * span - query_block * BLOCK

        def fill(i, count):
            block = pattern_ref[query_block, i]

            @pl.when(block >= 0)
            def _():
                for e in range(2):
                    unit = 2 * block + e
                    upper = unit >= n
                    device = owner[jnp.where(upper, 2 * n - 1 - unit, unit)]
                    row = pl.multiple_of(device * tok_rows + jnp.where(upper, span, 0), span)
                    to = pl.ds(pl.multiple_of(count * BLOCK + e * span, span), span)
                    for h in range(KVH):
                        for buf, col in ((kbuf, h * HD), (vbuf, (KVH + h) * HD)):
                            buf[h, to, :HD] = kv_ref[
                                col // width, pl.ds(row, span), col % width : col % width + HD
                            ]

            return count + (block >= 0).astype(jnp.int32)

        count = lax.fori_loop(0, slots, fill, jnp.int32(0))

        @pl.when(count % 2 == 1)
        def _():
            to = pl.ds(pl.multiple_of(count * BLOCK, BLOCK), BLOCK)
            kbuf[:, to, :] = jnp.zeros((KVH, BLOCK, HD), kbuf.dtype)
            vbuf[:, to, :HD] = jnp.zeros((KVH, BLOCK, HD), vbuf.dtype)

        chunks = (count + 1) // 2

        if scores.shape[0] > 4:
            attend_long(
                part, count, chunks, offset, span, group, rot_ref, kbuf, vbuf, scores, out_ref
            )
            continue

        line = offset + lax.broadcasted_iota(jnp.int32, (span, BLOCK), 0)
        col = lax.broadcasted_iota(jnp.int32, (span, BLOCK), 1)
        first_bias = jnp.where(col <= line, 0.0, MASKED)[None]
        last_bias = jnp.where(count % 2 == 1, MASKED, 0.0)

        for v in range(1, scores.shape[0] + 1):

            @pl.when(chunks == v)
            def _(v=v):
                def one_head(h, carry):
                    query = rot_ref[part, pl.ds(h * group, group)].reshape(rows, HD)
                    keys = kbuf[h, : v * CHUNK]
                    s = lax.dot_general(
                        query, keys, (((1,), (1,)), ((), ())), preferred_element_type=jnp.float32
                    )
                    front = s[:, :BLOCK].reshape(group, span, BLOCK) + first_bias
                    pieces = [front.reshape(rows, BLOCK)]
                    if v > 1:
                        pieces.append(s[:, BLOCK:-BLOCK])
                    pieces.append(s[:, -BLOCK:] + last_bias)
                    s = jnp.concatenate(pieces, axis=1)
                    top = jnp.max(s, axis=1, keepdims=True)
                    weights = jnp.exp2((s - top) * factor).astype(jnp.bfloat16)
                    total = jnp.dot(
                        weights, vbuf[h, : v * CHUNK], preferred_element_type=jnp.float32
                    )
                    result = (total[:, :HD] / total[:, HD:]).astype(jnp.bfloat16)
                    for j in range(group):
                        to = pl.ds(pl.multiple_of((h * group + j) * HD, HD), HD)
                        out_ref[part * span : (part + 1) * span, to] = result[
                            j * span : (j + 1) * span
                        ]
                    return carry

                lax.fori_loop(0, KVH, one_head, 0)


def attend(n, pattern, span_pairs, rotated, kv, tok_rows):
    span = tok_rows // 2
    chunks = (pattern.shape[1] + 1) // 2
    keys = chunks * CHUNK
    rows = QH // KVH * span
    smem = pl.BlockSpec(memory_space=pltpu.SMEM)
    vmem = pl.BlockSpec(memory_space=pltpu.VMEM)
    return pl.pallas_call(
        functools.partial(attend_kernel, n),
        out_shape=jax.ShapeDtypeStruct((tok_rows, QH * HD), jnp.bfloat16),
        in_specs=[smem, smem, vmem, vmem],
        out_specs=vmem,
        scratch_shapes=[
            pltpu.VMEM((KVH, keys, HD), jnp.bfloat16),
            pltpu.VMEM((KVH, keys, 2 * HD), jnp.bfloat16),
            pltpu.VMEM((chunks, rows, CHUNK), jnp.float32),
            pltpu.SMEM((n,), jnp.int32),
        ],
        compiler_params=pltpu.CompilerParams(vmem_limit_bytes=24 * 1024 * 1024),
    )(pattern, span_pairs, rotated, kv)


MESH = pl.DeviceIdType.MESH


def project_kernel(
    n,
    groups,
    weight_ref,
    hidden_ref,
    queries_ref,
    spans_ref,
    frequency_ref,
    rot_ref,
    kv_ref,
    weights,
    states,
    asked,
    tables,
    product,
    outgoing,
    sems,
    kv_sems,
    side_sems,
    kv_side_sems,
    own_sems,
    kv_own_sems,
    peer_sems,
    table_sems,
    kv_peer_sems,
    local_sems,
):
    g = lax.axis_index("groups")
    me = lax.axis_index("ctx")
    chips = n // 2
    half = chips // 2
    chip, core = me // 2, me % 2
    depth, width = weight_ref.shape[0], weights.shape[1]
    tok_rows = hidden_ref.shape[0]
    span = tok_rows // 2
    cut = depth // 2

    if chips > 8:
        spot = chip
    else:
        spot = (1 - chip % 2) * (chip // 2) + (chip % 2) * (chips - 1 - chip // 2)

    def index(position, which):
        p = (position + chips) % chips
        if chips > 8:
            return p * 2 + which
        back = p // half
        return 2 * ((1 - back) * 2 * p + back * (2 * (chips - 1 - p) + 1)) + which

    sibling = (g, chip * 2 + 1 - core)
    ring = ((g, index(spot + 1, core)), (g, index(spot - 1, core)))
    peers = [((g + d) % groups, me) for d in range(1, groups)]

    barrier = pltpu.get_barrier_semaphore()
    for device in (sibling, *ring, *peers):
        pl.semaphore_signal(barrier, inc=1, device_id=device, device_id_type=MESH)
    pl.semaphore_wait(barrier, 3 + len(peers))

    started = []

    def copy(source, target, send, receive, device):
        return pltpu.make_async_remote_copy(
            src_ref=source,
            dst_ref=target,
            send_sem=send,
            recv_sem=receive,
            device_id=device,
            device_id_type=MESH,
        )

    def send(*args):
        c = copy(*args)
        c.start()
        started.append(c)

    def gather(place, first, pieces, ready, ring_sems, across, own, between):
        def used(d, k, i):
            if k < half - 1:
                return True
            return (i < pieces // 2) == (d == 0)

        for i in range(pieces):
            ready(i)
            for d in range(2):
                if used(d, 0, i):
                    send(
                        first(i), place(me, i), ring_sems.at[0, d, 0, i],
                        ring_sems.at[1, d, 0, i], ring[d],
                    )
            send(first(i), place(me, i), own.at[0, i], own.at[1, i], sibling)
        between()
        for k in range(1, half + 1):
            for i in range(pieces):
                for d in range(2):
                    if not used(d, k - 1, i):
                        continue
                    at = place(index(spot - k if d == 0 else spot + k, core), i)
                    s, r = ring_sems.at[0, d, k - 1, i], ring_sems.at[1, d, k - 1, i]
                    copy(at, at, s, r, ring[d]).wait_recv()
                    if k < half and used(d, k, i):
                        send(at, at, ring_sems.at[0, d, k, i], ring_sems.at[1, d, k, i], ring[d])
                    send(at, at, across.at[0, d, k - 1, i], across.at[1, d, k - 1, i], sibling)
        for i in range(pieces):
            at = place(sibling[1], i)
            copy(at, at, own.at[0, i], own.at[1, i], sibling).wait_recv()
        for k in range(1, half + 1):
            for i in range(pieces):
                for d in range(2):
                    if used(d, k - 1, i):
                        at = place(index(spot - k if d == 0 else spot + k, 1 - core), i)
                        s, r = across.at[0, d, k - 1, i], across.at[1, d, k - 1, i]
                        copy(at, at, s, r, sibling).wait_recv()

    columns = pl.ds(pl.multiple_of(g * width, width), width)

    def weight_place(slot, i):
        return weights.at[pl.ds(pl.multiple_of(slot * depth + i * cut, cut), cut), :]

    locals_ = [
        pltpu.make_async_copy(
            weight_ref.at[:, columns],
            weights.at[pl.ds(pl.multiple_of(me * depth, depth), depth), :],
            local_sems.at[0],
        ),
        pltpu.make_async_copy(hidden_ref, states.at[g], local_sems.at[1]),
        pltpu.make_async_copy(queries_ref, asked, local_sems.at[2]),
    ]

    def between():
        for d, device in enumerate(peers):
            send(hidden_ref, states.at[g], peer_sems.at[0, d], peer_sems.at[1, d], device)
        for c in locals_:
            c.start()
        low = spans_ref[me]
        line = lax.broadcasted_iota(jnp.int32, (tok_rows, HD), 0)
        place = jnp.where(line < span, low * span, (2 * n - 2 - low) * span) + line
        angles = place.astype(jnp.float32) * frequency_ref[...]
        lane = lax.broadcasted_iota(jnp.int32, (tok_rows, HD), 1)
        sine = jnp.sin(angles)
        tables[g, 0] = jnp.cos(angles)
        tables[g, 1] = jnp.where(lane < HD // 2, -sine, sine)
        for d, device in enumerate(peers):
            send(
                tables.at[g], tables.at[g], table_sems.at[0, d], table_sems.at[1, d], device
            )
        for c in locals_:
            c.wait()

        def rotate(h, carry):
            x = asked[:, pl.ds(pl.multiple_of(h * HD, HD), HD)].astype(jnp.float32)
            y = x * tables[g, 0] + pltpu.roll(x, HD // 2, 1) * tables[g, 1]
            y = y.astype(jnp.bfloat16)
            rot_ref[0, h] = y[:span]
            rot_ref[1, h] = y[span:]
            return carry

        lax.fori_loop(0, QH, rotate, 0)

    gather(
        weight_place,
        lambda i: weight_ref.at[pl.ds(i * cut, cut), columns],
        2,
        lambda i: None,
        sems,
        side_sems,
        own_sems,
        between,
    )
    for d in range(groups - 1):
        source = (g + groups - 1 - d) % groups
        copy(
            states.at[source], states.at[source], peer_sems.at[0, d], peer_sems.at[1, d], peers[d]
        ).wait_recv()
        copy(
            tables.at[source], tables.at[source], table_sems.at[0, d], table_sems.at[1, d], peers[d]
        ).wait_recv()

    def multiply(c, carry):
        at = pl.ds(pl.multiple_of(c * CHUNK, CHUNK), CHUNK)
        x = states[...].reshape(groups * tok_rows, states.shape[2])
        product[:, :, at] = jnp.dot(
            x, weights[:, at], preferred_element_type=jnp.float32
        ).reshape(groups, tok_rows, CHUNK)
        return carry

    lax.fori_loop(0, width // CHUNK, multiply, 0)

    is_key = g * width < KVH * HD

    def finish(which, store):
        for h in range(width // HD):
            x = product[which, :, h * HD : (h + 1) * HD]
            y = x * tables[which, 0] + pltpu.roll(x, HD // 2, 1) * tables[which, 1]
            store(h, jnp.where(is_key, y, x).astype(jnp.bfloat16))

    def store_own(h, value):
        kv_ref[g, me, :, h * HD : (h + 1) * HD] = value

    finish(g, store_own)

    def share():
        for d, device in enumerate(peers):

            def store(h, value, d=d):
                outgoing[d, :, h * HD : (h + 1) * HD] = value

            finish(device[0], store)
            send(
                outgoing.at[d], kv_ref.at[g, me], kv_peer_sems.at[0, d], kv_peer_sems.at[1, d],
                device,
            )

    def kv_place(slot, i):
        return kv_ref.at[(g + i) % groups, slot]

    def ready(i):
        if i == 1:
            share()
        if i:
            at = kv_place(me, i)
            d = groups - i - 1
            copy(at, at, kv_peer_sems.at[0, d], kv_peer_sems.at[1, d], peers[d]).wait_recv()

    gather(
        kv_place,
        lambda i: kv_place(me, i),
        groups,
        ready,
        kv_sems,
        kv_side_sems,
        kv_own_sems,
        lambda: None,
    )
    for c in started:
        c.wait_send()


def project(n, groups, weight, hidden, queries, span_pairs):
    depth, width = weight.shape[0], weight.shape[1] // groups
    tok_rows, wide = hidden.shape
    half = n // 4
    half_ids = jnp.arange(HD // 2, dtype=jnp.float32)
    frequency = ROPE_BASE ** (-(half_ids * 2.0 / HD))
    frequency = jnp.concatenate([frequency, frequency])[None]
    hbm = pl.BlockSpec(memory_space=pltpu.HBM)
    smem = pl.BlockSpec(memory_space=pltpu.SMEM)
    vmem = pl.BlockSpec(memory_space=pltpu.VMEM)
    dma = pltpu.SemaphoreType.DMA
    weight, hidden, queries = (
        pltpu.with_memory_space_constraint(x, pltpu.HBM) for x in (weight, hidden, queries)
    )
    return pl.pallas_call(
        functools.partial(project_kernel, n, groups),
        out_shape=(
            jax.ShapeDtypeStruct((2, QH, tok_rows // 2, HD), jnp.bfloat16),
            jax.ShapeDtypeStruct((groups, n, tok_rows, width), jnp.bfloat16),
        ),
        in_specs=[hbm, hbm, hbm, smem, vmem],
        out_specs=(vmem, vmem),
        scratch_shapes=[
            pltpu.VMEM((n * depth, width), jnp.bfloat16),
            pltpu.VMEM((groups, tok_rows, wide), jnp.bfloat16),
            pltpu.VMEM(queries.shape, jnp.bfloat16),
            pltpu.VMEM((groups, 2, tok_rows, HD), jnp.float32),
            pltpu.VMEM((groups, tok_rows, width), jnp.float32),
            pltpu.VMEM((groups - 1, tok_rows, width), jnp.bfloat16),
            dma((2, 2, half, 2)),
            dma((2, 2, half, groups)),
            dma((2, 2, half, 2)),
            dma((2, 2, half, groups)),
            dma((2, 2)),
            dma((2, groups)),
            dma((2, groups - 1)),
            dma((2, groups - 1)),
            dma((2, groups - 1)),
            dma((3,)),
        ],
        compiler_params=pltpu.CompilerParams(
            collective_id=0, has_side_effects=True, vmem_limit_bytes=24 * 1024 * 1024
        ),
    )(weight, hidden, queries, span_pairs, frequency)


def body(groups, hidden, queries, cache_weight, pattern, span_pairs):
    tok_rows = hidden.shape[0]
    n = lax.axis_size("ctx")
    rotated, kv = project(n, groups, cache_weight, hidden, queries, span_pairs)
    kv = kv.reshape(groups, n * tok_rows, kv.shape[3])
    return attend(n, pattern, span_pairs, rotated, kv, tok_rows)


def solution(mesh):
    in_specs = (
        P(("groups", "ctx"), None),
        P(("groups", "ctx"), None),
        P("ctx", None),
        P("groups", None),
        P("groups"),
    )
    return jax.shard_map(
        functools.partial(body, mesh.shape["groups"]),
        mesh=mesh,
        in_specs=in_specs,
        out_specs=P(("groups", "ctx"), None),
        check_vma=False,
    )
```

```python
import functools
import math

import jax
import jax.numpy as jnp
from jax import lax
from jax.experimental import pallas as pl
from jax.experimental.pallas import tpu as pltpu
from jax.sharding import PartitionSpec as P

QH = 32
KVH = 4
HD = 128
BLOCK = 128
ROPE_BASE = 500000.0
MASKED = -1e30
CHUNK = 2 * BLOCK


def attend_long(part, count, chunks, offset, span, group, rot_ref, kbuf, vbuf, scores, out_ref):
    rows = group * span
    factor = HD ** (-0.5) * math.log2(math.e)
    for h in range(KVH):
        query = rot_ref[part, h * group : (h + 1) * group].reshape(rows, HD)

        def score(c, peak):
            keys = kbuf[h, pl.ds(pl.multiple_of(c * CHUNK, CHUNK), CHUNK), :]
            s = lax.dot_general(
                query, keys, (((1,), (1,)), ((), ())), preferred_element_type=jnp.float32
            )
            col = c * CHUNK + lax.broadcasted_iota(jnp.int32, (span, CHUNK), 1)
            line = offset + lax.broadcasted_iota(jnp.int32, (span, CHUNK), 0)
            live = (col < count * BLOCK) & ((col >= BLOCK) | (col <= line))
            bias = jnp.where(live, 0.0, MASKED)
            s = (s.reshape(group, span, CHUNK) + bias[None]).reshape(rows, CHUNK)
            scores[c] = s
            return jnp.maximum(peak, jnp.maximum(s[:, :BLOCK], s[:, BLOCK:]))

        peak = lax.fori_loop(
            0, chunks, score, jnp.full((rows, BLOCK), MASKED, jnp.float32)
        )
        top = jnp.max(peak, axis=1, keepdims=True)

        def mix(c, total):
            weights = jnp.exp2((scores[c] - top) * factor).astype(jnp.bfloat16)
            values = vbuf[h, pl.ds(pl.multiple_of(c * CHUNK, CHUNK), CHUNK), :]
            return total + jnp.dot(weights, values, preferred_element_type=jnp.float32)

        total = lax.fori_loop(0, chunks, mix, jnp.zeros((rows, 2 * HD), jnp.float32))
        result = (total[:, :HD] / total[:, HD:]).astype(jnp.bfloat16)
        for j in range(group):
            head = h * group + j
            out_ref[part * span : (part + 1) * span, head * HD : (head + 1) * HD] = result[
                j * span : (j + 1) * span
            ]


def attend_kernel(
    n, pattern_ref, spans_ref, rot_ref, kv_ref, out_ref, kbuf, vbuf, scores, owner
):
    me = lax.axis_index("ctx")
    tok_rows = out_ref.shape[0]
    span = tok_rows // 2
    width = kv_ref.shape[2]
    group = QH // KVH
    rows = group * span
    slots = pattern_ref.shape[1]
    factor = HD ** (-0.5) * math.log2(math.e)

    def place(d, carry):
        owner[spans_ref[d]] = d
        return carry

    lax.fori_loop(0, n, place, 0)
    vbuf[:, :, HD:] = jnp.ones_like(vbuf[:, :, HD:])
    low = spans_ref[me]

    for part in range(2):
        span_id = low if part == 0 else 2 * n - 1 - low
        query_block = span_id * span // BLOCK
        offset = span_id * span - query_block * BLOCK

        def fill(i, count):
            block = pattern_ref[query_block, i]

            @pl.when(block >= 0)
            def _():
                for e in range(2):
                    unit = 2 * block + e
                    upper = unit >= n
                    device = owner[jnp.where(upper, 2 * n - 1 - unit, unit)]
                    row = pl.multiple_of(device * tok_rows + jnp.where(upper, span, 0), span)
                    to = pl.ds(pl.multiple_of(count * BLOCK + e * span, span), span)
                    for h in range(KVH):
                        for buf, col in ((kbuf, h * HD), (vbuf, (KVH + h) * HD)):
                            buf[h, to, :HD] = kv_ref[
                                col // width, pl.ds(row, span), col % width : col % width + HD
                            ]

            return count + (block >= 0).astype(jnp.int32)

        count = lax.fori_loop(0, slots, fill, jnp.int32(0))

        @pl.when(count % 2 == 1)
        def _():
            to = pl.ds(pl.multiple_of(count * BLOCK, BLOCK), BLOCK)
            kbuf[:, to, :] = jnp.zeros((KVH, BLOCK, HD), kbuf.dtype)
            vbuf[:, to, :HD] = jnp.zeros((KVH, BLOCK, HD), vbuf.dtype)

        chunks = (count + 1) // 2

        if scores.shape[0] > 4:
            attend_long(
                part, count, chunks, offset, span, group, rot_ref, kbuf, vbuf, scores, out_ref
            )
            continue

        line = offset + lax.broadcasted_iota(jnp.int32, (span, BLOCK), 0)
        col = lax.broadcasted_iota(jnp.int32, (span, BLOCK), 1)
        first_bias = jnp.where(col <= line, 0.0, MASKED)[None]
        last_bias = jnp.where(count % 2 == 1, MASKED, 0.0)

        for v in range(1, scores.shape[0] + 1):

            @pl.when(chunks == v)
            def _(v=v):
                def one_head(h, carry):
                    query = rot_ref[part, pl.ds(h * group, group)].reshape(rows, HD)
                    keys = kbuf[h, : v * CHUNK]
                    s = lax.dot_general(
                        query, keys, (((1,), (1,)), ((), ())), preferred_element_type=jnp.float32
                    )
                    front = s[:, :BLOCK].reshape(group, span, BLOCK) + first_bias
                    pieces = [front.reshape(rows, BLOCK)]
                    if v > 1:
                        pieces.append(s[:, BLOCK:-BLOCK])
                    pieces.append(s[:, -BLOCK:] + last_bias)
                    s = jnp.concatenate(pieces, axis=1)
                    top = jnp.max(s, axis=1, keepdims=True)
                    weights = jnp.exp2((s - top) * factor).astype(jnp.bfloat16)
                    total = jnp.dot(
                        weights, vbuf[h, : v * CHUNK], preferred_element_type=jnp.float32
                    )
                    result = (total[:, :HD] / total[:, HD:]).astype(jnp.bfloat16)
                    for j in range(group):
                        to = pl.ds(pl.multiple_of((h * group + j) * HD, HD), HD)
                        out_ref[part * span : (part + 1) * span, to] = result[
                            j * span : (j + 1) * span
                        ]
                    return carry

                lax.fori_loop(0, KVH, one_head, 0, unroll=2)


def attend(n, pattern, span_pairs, rotated, kv, tok_rows):
    span = tok_rows // 2
    chunks = (pattern.shape[1] + 1) // 2
    keys = chunks * CHUNK
    rows = QH // KVH * span
    smem = pl.BlockSpec(memory_space=pltpu.SMEM)
    vmem = pl.BlockSpec(memory_space=pltpu.VMEM)
    return pl.pallas_call(
        functools.partial(attend_kernel, n),
        out_shape=jax.ShapeDtypeStruct((tok_rows, QH * HD), jnp.bfloat16),
        in_specs=[smem, smem, vmem, vmem],
        out_specs=vmem,
        scratch_shapes=[
            pltpu.VMEM((KVH, keys, HD), jnp.bfloat16),
            pltpu.VMEM((KVH, keys, 2 * HD), jnp.bfloat16),
            pltpu.VMEM((chunks, rows, CHUNK), jnp.float32),
            pltpu.SMEM((n,), jnp.int32),
        ],
        compiler_params=pltpu.CompilerParams(vmem_limit_bytes=24 * 1024 * 1024),
    )(pattern, span_pairs, rotated, kv)


MESH = pl.DeviceIdType.MESH


def project_kernel(
    n,
    groups,
    weight_ref,
    hidden_ref,
    queries_ref,
    spans_ref,
    frequency_ref,
    rot_ref,
    kv_ref,
    weights,
    states,
    asked,
    tables,
    product,
    outgoing,
    sems,
    kv_sems,
    side_sems,
    kv_side_sems,
    own_sems,
    kv_own_sems,
    peer_sems,
    table_sems,
    kv_peer_sems,
    local_sems,
):
    g = lax.axis_index("groups")
    me = lax.axis_index("ctx")
    chips = n // 2
    half = chips // 2
    chip, core = me // 2, me % 2
    depth, width = weight_ref.shape[0], weights.shape[1]
    tok_rows = hidden_ref.shape[0]
    span = tok_rows // 2
    cut = depth // 2

    if chips > 8:
        spot = chip
    else:
        spot = (1 - chip % 2) * (chip // 2) + (chip % 2) * (chips - 1 - chip // 2)

    def index(position, which):
        p = (position + chips) % chips
        if chips > 8:
            return p * 2 + which
        back = p // half
        return 2 * ((1 - back) * 2 * p + back * (2 * (chips - 1 - p) + 1)) + which

    sibling = (g, chip * 2 + 1 - core)
    ring = ((g, index(spot + 1, core)), (g, index(spot - 1, core)))
    peers = [((g + d) % groups, me) for d in range(1, groups)]

    barrier = pltpu.get_barrier_semaphore()
    for device in (sibling, *ring, *peers):
        pl.semaphore_signal(barrier, inc=1, device_id=device, device_id_type=MESH)
    pl.semaphore_wait(barrier, 3 + len(peers))

    started = []

    def copy(source, target, send, receive, device):
        return pltpu.make_async_remote_copy(
            src_ref=source,
            dst_ref=target,
            send_sem=send,
            recv_sem=receive,
            device_id=device,
            device_id_type=MESH,
        )

    def send(*args):
        c = copy(*args)
        c.start()
        started.append(c)

    def gather(place, first, pieces, ready, ring_sems, across, own, between):
        def used(d, k, i):
            if k < half - 1:
                return True
            return (i < pieces // 2) == (d == 0)

        for i in range(pieces):
            ready(i)
            for d in range(2):
                if used(d, 0, i):
                    send(
                        first(i), place(me, i), ring_sems.at[0, d, 0, i],
                        ring_sems.at[1, d, 0, i], ring[d],
                    )
            send(first(i), place(me, i), own.at[0, i], own.at[1, i], sibling)
        between()
        for k in range(1, half + 1):
            for i in range(pieces):
                for d in range(2):
                    if not used(d, k - 1, i):
                        continue
                    at = place(index(spot - k if d == 0 else spot + k, core), i)
                    s, r = ring_sems.at[0, d, k - 1, i], ring_sems.at[1, d, k - 1, i]
                    copy(at, at, s, r, ring[d]).wait_recv()
                    if k < half and used(d, k, i):
                        send(at, at, ring_sems.at[0, d, k, i], ring_sems.at[1, d, k, i], ring[d])
                    send(at, at, across.at[0, d, k - 1, i], across.at[1, d, k - 1, i], sibling)
        for i in range(pieces):
            at = place(sibling[1], i)
            copy(at, at, own.at[0, i], own.at[1, i], sibling).wait_recv()
        for k in range(1, half + 1):
            for i in range(pieces):
                for d in range(2):
                    if used(d, k - 1, i):
                        at = place(index(spot - k if d == 0 else spot + k, 1 - core), i)
                        s, r = across.at[0, d, k - 1, i], across.at[1, d, k - 1, i]
                        copy(at, at, s, r, sibling).wait_recv()

    columns = pl.ds(pl.multiple_of(g * width, width), width)

    def weight_place(slot, i):
        return weights.at[pl.ds(pl.multiple_of(slot * depth + i * cut, cut), cut), :]

    locals_ = [
        pltpu.make_async_copy(
            weight_ref.at[:, columns],
            weights.at[pl.ds(pl.multiple_of(me * depth, depth), depth), :],
            local_sems.at[0],
        ),
        pltpu.make_async_copy(hidden_ref, states.at[g], local_sems.at[1]),
        pltpu.make_async_copy(queries_ref, asked, local_sems.at[2]),
    ]

    def between():
        for d, device in enumerate(peers):
            send(hidden_ref, states.at[g], peer_sems.at[0, d], peer_sems.at[1, d], device)
        for c in locals_:
            c.start()
        low = spans_ref[me]
        line = lax.broadcasted_iota(jnp.int32, (tok_rows, HD), 0)
        place = jnp.where(line < span, low * span, (2 * n - 2 - low) * span) + line
        angles = place.astype(jnp.float32) * frequency_ref[...]
        lane = lax.broadcasted_iota(jnp.int32, (tok_rows, HD), 1)
        sine = jnp.sin(angles)
        tables[g, 0] = jnp.cos(angles)
        tables[g, 1] = jnp.where(lane < HD // 2, -sine, sine)
        for d, device in enumerate(peers):
            send(
                tables.at[g], tables.at[g], table_sems.at[0, d], table_sems.at[1, d], device
            )
        for c in locals_:
            c.wait()

        def rotate(h, carry):
            x = asked[:, pl.ds(pl.multiple_of(h * HD, HD), HD)].astype(jnp.float32)
            y = x * tables[g, 0] + pltpu.roll(x, HD // 2, 1) * tables[g, 1]
            y = y.astype(jnp.bfloat16)
            rot_ref[0, h] = y[:span]
            rot_ref[1, h] = y[span:]
            return carry

        lax.fori_loop(0, QH, rotate, 0)

    gather(
        weight_place,
        lambda i: weight_ref.at[pl.ds(i * cut, cut), columns],
        2,
        lambda i: None,
        sems,
        side_sems,
        own_sems,
        between,
    )
    for d in range(groups - 1):
        source = (g + groups - 1 - d) % groups
        copy(
            states.at[source], states.at[source], peer_sems.at[0, d], peer_sems.at[1, d], peers[d]
        ).wait_recv()
        copy(
            tables.at[source], tables.at[source], table_sems.at[0, d], table_sems.at[1, d], peers[d]
        ).wait_recv()

    def multiply(c, carry):
        at = pl.ds(pl.multiple_of(c * CHUNK, CHUNK), CHUNK)
        x = states[...].reshape(groups * tok_rows, states.shape[2])
        product[:, :, at] = jnp.dot(
            x, weights[:, at], preferred_element_type=jnp.float32
        ).reshape(groups, tok_rows, CHUNK)
        return carry

    lax.fori_loop(0, width // CHUNK, multiply, 0)

    is_key = g * width < KVH * HD

    def finish(which, store):
        for h in range(width // HD):
            x = product[which, :, h * HD : (h + 1) * HD]
            y = x * tables[which, 0] + pltpu.roll(x, HD // 2, 1) * tables[which, 1]
            store(h, jnp.where(is_key, y, x).astype(jnp.bfloat16))

    def store_own(h, value):
        kv_ref[g, me, :, h * HD : (h + 1) * HD] = value

    finish(g, store_own)

    def share():
        for d, device in enumerate(peers):

            def store(h, value, d=d):
                outgoing[d, :, h * HD : (h + 1) * HD] = value

            finish(device[0], store)
            send(
                outgoing.at[d], kv_ref.at[g, me], kv_peer_sems.at[0, d], kv_peer_sems.at[1, d],
                device,
            )

    def kv_place(slot, i):
        return kv_ref.at[(g + i) % groups, slot]

    def ready(i):
        if i == 1:
            share()
        if i:
            at = kv_place(me, i)
            d = groups - i - 1
            copy(at, at, kv_peer_sems.at[0, d], kv_peer_sems.at[1, d], peers[d]).wait_recv()

    gather(
        kv_place,
        lambda i: kv_place(me, i),
        groups,
        ready,
        kv_sems,
        kv_side_sems,
        kv_own_sems,
        lambda: None,
    )
    for c in started:
        c.wait_send()


def project(n, groups, weight, hidden, queries, span_pairs):
    depth, width = weight.shape[0], weight.shape[1] // groups
    tok_rows, wide = hidden.shape
    half = n // 4
    half_ids = jnp.arange(HD // 2, dtype=jnp.float32)
    frequency = ROPE_BASE ** (-(half_ids * 2.0 / HD))
    frequency = jnp.concatenate([frequency, frequency])[None]
    hbm = pl.BlockSpec(memory_space=pltpu.HBM)
    smem = pl.BlockSpec(memory_space=pltpu.SMEM)
    vmem = pl.BlockSpec(memory_space=pltpu.VMEM)
    dma = pltpu.SemaphoreType.DMA
    weight, hidden, queries = (
        pltpu.with_memory_space_constraint(x, pltpu.HBM) for x in (weight, hidden, queries)
    )
    return pl.pallas_call(
        functools.partial(project_kernel, n, groups),
        out_shape=(
            jax.ShapeDtypeStruct((2, QH, tok_rows // 2, HD), jnp.bfloat16),
            jax.ShapeDtypeStruct((groups, n, tok_rows, width), jnp.bfloat16),
        ),
        in_specs=[hbm, hbm, hbm, smem, vmem],
        out_specs=(vmem, vmem),
        scratch_shapes=[
            pltpu.VMEM((n * depth, width), jnp.bfloat16),
            pltpu.VMEM((groups, tok_rows, wide), jnp.bfloat16),
            pltpu.VMEM(queries.shape, jnp.bfloat16),
            pltpu.VMEM((groups, 2, tok_rows, HD), jnp.float32),
            pltpu.VMEM((groups, tok_rows, width), jnp.float32),
            pltpu.VMEM((groups - 1, tok_rows, width), jnp.bfloat16),
            dma((2, 2, half, 2)),
            dma((2, 2, half, groups)),
            dma((2, 2, half, 2)),
            dma((2, 2, half, groups)),
            dma((2, 2)),
            dma((2, groups)),
            dma((2, groups - 1)),
            dma((2, groups - 1)),
            dma((2, groups - 1)),
            dma((3,)),
        ],
        compiler_params=pltpu.CompilerParams(
            collective_id=0, has_side_effects=True, vmem_limit_bytes=24 * 1024 * 1024
        ),
    )(weight, hidden, queries, span_pairs, frequency)


def body(groups, hidden, queries, cache_weight, pattern, span_pairs):
    tok_rows = hidden.shape[0]
    n = lax.axis_size("ctx")
    rotated, kv = project(n, groups, cache_weight, hidden, queries, span_pairs)
    kv = kv.reshape(groups, n * tok_rows, kv.shape[3])
    return attend(n, pattern, span_pairs, rotated, kv, tok_rows)


def solution(mesh):
    in_specs = (
        P(("groups", "ctx"), None),
        P(("groups", "ctx"), None),
        P("ctx", None),
        P("groups", None),
        P("groups"),
    )
    return jax.shard_map(
        functools.partial(body, mesh.shape["groups"]),
        mesh=mesh,
        in_specs=in_specs,
        out_specs=P(("groups", "ctx"), None),
        check_vma=False,
    )
```
